128 devices in a mesh: slot: 32 (over z, x, core), grp: 4 (over y).
Axes of the slice: x: 4, y: 4, z: 4, core: 2. Of those that a mesh axis runs over, the one named last changes fastest.
Arguments:
- token_rows: bfloat16 [2, 32, 4, 384, 2048], P(None, 'slot', 'grp'), may hold values from -6 to 6
- cotangents: bfloat16 [2, 32, 4, 384, 2048], P(None, 'slot', 'grp'), may hold values from -6 to 6
- row_counts: int32 [2, 32, 4], P(None, 'slot', 'grp'), may hold values from 96 to 384, as said below
- old_place: int32 [32, 4], replicated, may hold values from 0 to 3, as said below
- new_place: int32 [32, 4], replicated, may hold values from 0 to 3, as said below
- momentum: float32 [16, 3145728], P(None, ('slot', 'grp')), may hold values from -4 to 4
- curvature: float32 [16, 3145728], P(None, ('slot', 'grp')), may hold values from 0.01 to 1
- master: float32 [16, 3145728], P(None, ('slot', 'grp')), may hold values from -0.125 to 0.125
Outputs:
- d_rows: bfloat16 [2, 32, 4, 384, 2048], P(None, 'slot', 'grp')
- momentum_out: float32 [16, 3145728], P(None, ('slot', 'grp'))
- curvature_out: float32 [16, 3145728], P(None, ('slot', 'grp'))
- master_out: float32 [16, 3145728], P(None, ('slot', 'grp'))
The draws below stay inside these ranges and needn't reach their ends.
Inputs may be any that keep to these rules, and one draw needn't show every extreme that they name: `old_place`: entry [s, g] is the expert, numbered within group g, held by slot s of group g; each of the 4 experts of every group has at least one slot. `new_place`: entry [s, g] is the expert, numbered within group g, held by slot s of group g; each of the 4 experts of every group has at least one slot. `row_counts`: rows from this count on are padding; in each step some slot has exactly 384 live rows.
All inputs are finite; a program needn't handle non-finite values.
Results may differ from the reference program's by a relative error of at most 0.0074.
Values may be sent and summed in bfloat16 or wider, within the bound.
No kernel may reach another device: no remote copies, remote signals or barrier semaphores. Data moves between devices by JAX's collectives and lax.ppermute only.
A program may use at most 128 MiB of HBM per device.

```python
import math
import jax
import jax.numpy as jnp
from jax import lax

D = 2048
FF = 512
CAP = 384
EXP_GRP = 4
STEPS = 2
SLOTS = 32
GROUPS = 4
EXPERTS = 16
PARAMS = 3145728


def place_draw(key):
    key_list = jax.random.split(key, 3)
    slot_order = jax.vmap(lambda subkey: jax.random.permutation(subkey, SLOTS))(jax.random.split(key_list[0], GROUPS))
    expert_order = jax.vmap(lambda subkey: jax.random.permutation(subkey, EXP_GRP))(jax.random.split(key_list[1], GROUPS))
    slot_rank = jnp.argsort(slot_order, axis=1).astype(jnp.int32)
    tickets = jax.random.randint(key_list[2], (GROUPS, SLOTS), 0, 2 ** EXP_GRP - 1)
    bounds = 2 ** jnp.arange(1, EXP_GRP, dtype=jnp.int32) - 1
    tier_index = jnp.sum((tickets[:, :, None] >= bounds[None, None, :]).astype(jnp.int32), axis=2)
    drawn_expert = jnp.take_along_axis(expert_order, tier_index, axis=1)
    fixed_expert = jnp.take_along_axis(expert_order, jnp.minimum(slot_rank, EXP_GRP - 1), axis=1)
    chosen = jnp.where(slot_rank < EXP_GRP, fixed_expert, drawn_expert)
    return chosen.T.astype(jnp.int32)


def draw_old_place(key, part):
    return place_draw(jax.random.fold_in(key, 11))


def draw_new_place(key, part):
    return place_draw(jax.random.fold_in(key, 12))


def draw_row_counts(key, part):
    first, second = jax.random.split(jax.random.fold_in(key, 31))
    counts = jax.random.randint(first, (STEPS, SLOTS * GROUPS), CAP // 4, CAP + 1)
    full_slot = jax.random.randint(second, (STEPS, 1), 0, SLOTS * GROUPS)
    chosen = jnp.arange(SLOTS * GROUPS, dtype=jnp.int32)[None, :] == full_slot
    return jnp.where(chosen, CAP, counts).reshape(STEPS, SLOTS, GROUPS).astype(jnp.int32)


def block_scale(key, extent, pieces, smallest, high):
    loudness = 1.0
    for dim, parts in pieces:
        steps = jax.random.uniform(jax.random.fold_in(jax.random.fold_in(key, 6), dim), (parts,), jnp.float32, smallest / len(pieces), high / len(pieces))
        loudness = loudness * jnp.repeat(jnp.exp(steps), extent[dim] // parts).reshape((-1,) + (1,) * (len(extent) - 1 - dim))
    return loudness


def normal_values(stream_key, shape, spread, limit, cuts=(), kind=jnp.bfloat16):
    drawn = jax.random.normal(stream_key, shape, jnp.float32) * spread
    if len(cuts) > 0:
        drawn = block_scale(stream_key, shape, cuts, -0.22, 0.18) * drawn
    return jnp.clip(drawn, min=-limit, max=limit).astype(kind)


def setup_inputs(seed: int = 0) -> dict:
    splits = jax.random.split(jax.random.key(seed), 9)
    token_rows = normal_values(splits[0], (STEPS, SLOTS, GROUPS, CAP, D), 1.0, 6.0, ((1, 32), (2, 4)))
    cotangents = normal_values(splits[1], (STEPS, SLOTS, GROUPS, CAP, D), 1.0, 6.0, ((1, 32), (2, 4)))
    row_counts = draw_row_counts(jax.random.fold_in(splits[8], 71), 0)
    old_place = draw_old_place(jax.random.fold_in(splits[8], 71), 0)
    new_place = draw_new_place(jax.random.fold_in(splits[8], 71), 0)
    momentum = normal_values(splits[5], (EXPERTS, PARAMS), 0.5, 4.0, ((1, 128),), jnp.float32)
    curvature = jnp.clip(jnp.exp(math.log(1.0) - 4.6051702 * jax.random.uniform(splits[6], (EXPERTS, PARAMS), jnp.float32) ** block_scale(splits[6], (EXPERTS, PARAMS), ((1, 128),), -0.2, 0.2)), 0.01, 1.0)
    master = normal_values(splits[7], (EXPERTS, PARAMS), D ** -0.5, 0.125, ((1, 128),), jnp.float32)
    return {"token_rows": token_rows, "cotangents": cotangents, "row_counts": row_counts, "old_place": old_place, "new_place": new_place, "momentum": momentum, "curvature": curvature, "master": master}


beta_one = 0.9
beta_two = 0.99
rho_scale = 2.0
learn_rate = 0.005
grad_scale = 0.25


def silu_parts(values):
    sigmoid = jax.nn.sigmoid(values)
    return values * sigmoid, sigmoid * (1.0 + values * (1.0 - sigmoid))


def slot_backward(rows_one, cotangent, live_count, flat_weights):
    split_at = 2 * D * FF
    w_gateup = flat_weights[:split_at].reshape(D, 2 * FF)
    w_down = flat_weights[split_at:].reshape(FF, D)
    live = (jnp.arange(rows_one.shape[0], dtype=jnp.int32) < live_count)[:, None]
    masked_ct = jnp.where(live, cotangent, jnp.zeros_like(cotangent))
    preact = jnp.dot(rows_one, w_gateup, preferred_element_type=jnp.float32)
    gate_pre = preact[:, :FF]
    up_pre = preact[:, FF:]
    activated, slope = silu_parts(gate_pre)
    hidden = (activated * up_pre).astype(jnp.bfloat16)
    hidden_grad = lax.dot_general(masked_ct, w_down, (((1,), (1,)), ((), ())), preferred_element_type=jnp.float32)
    pre_grad = jnp.concatenate([hidden_grad * up_pre * slope, hidden_grad * activated], axis=1).astype(jnp.bfloat16)
    row_grad = lax.dot_general(pre_grad, w_gateup, (((1,), (1,)), ((), ())), preferred_element_type=jnp.float32).astype(jnp.bfloat16)
    grad_gateup = lax.dot_general(rows_one, pre_grad, (((0,), (0,)), ((), ())), preferred_element_type=jnp.float32)
    grad_down = lax.dot_general(hidden, masked_ct, (((0,), (0,)), ((), ())), preferred_element_type=jnp.float32)
    return row_grad, jnp.concatenate([grad_gateup.reshape(-1), grad_down.reshape(-1)])


def sophia(grads, momentum, curvature, master):
    momentum = beta_one * momentum + (1.0 - beta_one) * grads
    curvature = beta_two * curvature + (1.0 - beta_two) * grads * grads
    master = master - learn_rate * jnp.clip(momentum / (rho_scale * curvature), -1.0, 1.0)
    return momentum, curvature, master


def reference(token_rows, cotangents, row_counts, old_place, new_place, momentum, curvature, master):
    owners = (jnp.arange(GROUPS, dtype=jnp.int32) * EXP_GRP)[None, :]
    outputs = []
    for step_index, place_map in ((0, old_place), (1, new_place)):
        expert_ids = (place_map + owners).reshape(-1).astype(jnp.int32)
        weights_bf = master.astype(jnp.bfloat16)
        rows_all = token_rows[step_index].reshape(SLOTS * GROUPS, CAP, D)
        ct_all = cotangents[step_index].reshape(SLOTS * GROUPS, CAP, D)
        counts_all = row_counts[step_index].reshape(-1)

        def per_slot(totals, items):
            rows_one, ct_one, count_one, expert_one = items
            flat = lax.dynamic_index_in_dim(weights_bf, expert_one, 0, keepdims=False)
            row_grad, flat_grad = slot_backward(rows_one, ct_one, count_one, flat)
            current = lax.dynamic_index_in_dim(totals, expert_one, 0, keepdims=False)
            totals = lax.dynamic_update_index_in_dim(totals, current + flat_grad, expert_one, 0)
            return totals, row_grad

        totals, row_grads = lax.scan(per_slot, jnp.zeros((EXPERTS, PARAMS), jnp.float32), (rows_all, ct_all, counts_all, expert_ids))
        momentum, curvature, master = sophia(totals * grad_scale, momentum, curvature, master)
        outputs.append(row_grads.reshape(SLOTS, GROUPS, CAP, D))
    return jnp.stack(outputs), momentum, curvature, master
```

```python
import jax
import jax.numpy as jnp
from jax import lax
from jax.experimental import pallas as pl
from jax.experimental.pallas import tpu as pltpu
from jax.sharding import PartitionSpec as P

D = 2048
FF = 512
ROWS = 384
WIDE = 1024
BLK = 96
NBLK = 32
PIECE = 24
SPLIT = 21
HEAD = 32

beta_one = 0.9
beta_two = 0.99
rho_scale = 2.0
learn_rate = 0.005
grad_scale = 0.25

F32 = jnp.float32
BF16 = jnp.bfloat16
VMEM = pltpu.VMEM
SMEM = pltpu.SMEM


def params(limit_mb, **more):
    return pltpu.CompilerParams(vmem_limit_bytes=limit_mb * 1024 * 1024, **more)


def wire_row(block, local):
    base = jnp.where(block == SPLIT, HEAD, 0)
    half = jnp.where(block == SPLIT, (BLK - HEAD) // 2, BLK // 2)
    inner = local - base
    moved = base + lax.rem(inner, 2) * half + lax.div(inner, 2)
    is_down = (block > SPLIT) | ((block == SPLIT) & (local >= HEAD))
    return jnp.where(is_down, moved, local)


def pack_kernel(where_ref, place_ref, p0, p1, p2, p3, out_ref, f32_ref, rows_ref, bf_ref, sem):
    block = where_ref[0]
    group = where_ref[1]
    for shift, piece in enumerate((p0, p1, p2, p3)):
        f32_ref[...] = piece[...].astype(F32)
        source = lax.rem(group - shift + 4, 4)

        for j in range(PIECE):
            row = wire_row(block, PIECE * source + j)
            for e in range(4):
                rows_ref[e, pl.ds(row, 1), :] = f32_ref[e : e + 1, j * WIDE : (j + 1) * WIDE]
    bf_ref[...] = rows_ref[...].astype(BF16)

    @pl.loop(0, NBLK)
    def _(s):
        pltpu.make_async_copy(bf_ref.at[place_ref[s]], out_ref.at[s], sem).start()

    pltpu.make_async_copy(out_ref, out_ref, sem).wait()


def pack(where, place, pieces):
    return pl.pallas_call(
        pack_kernel,
        out_shape=jax.ShapeDtypeStruct((NBLK, BLK, WIDE), BF16),
        in_specs=[pl.BlockSpec(memory_space=SMEM)] * 2 + [pl.BlockSpec(memory_space=VMEM)] * 4,
        out_specs=pl.BlockSpec(memory_space=pl.ANY),
        scratch_shapes=[
            VMEM((4, PIECE * WIDE), F32),
            VMEM((4, BLK, WIDE), F32),
            VMEM((4, BLK, WIDE), BF16),
            pltpu.SemaphoreType.DMA,
        ],
        compiler_params=params(32),
        name="pack",
    )(where, place, *pieces)


def down_spans():
    first = SPLIT * BLK + HEAD
    count = (BLK - HEAD) // 2
    spans = [(0, count, first, first + count)]
    done = count
    for block in range(SPLIT + 1, NBLK):
        spans.append((done, BLK // 2, block * BLK, block * BLK + BLK // 2))
        done += BLK // 2
    return spans


NT = (((1,), (1,)), ((), ()))
NN = (((1,), (0,)), ((), ()))


def dot(a, b, dims):
    return lax.dot_general(a, b, dims, preferred_element_type=F32)


def expert_kernel(count_ref, x_ref, xt_ref, dy_ref, w_ref, g_ref, dz_ref, dym_ref, wd_ref, h_ref, ht_ref):
    live = lax.broadcasted_iota(jnp.int32, (ROWS, 1), 0) < count_ref[0]
    dym_ref[...] = jnp.where(live, dy_ref[...], jnp.zeros((), BF16))
    for first, count, left, right in down_spans():
        wd_ref[first : first + count, :WIDE] = w_ref[left : left + count, :]
        wd_ref[first : first + count, WIDE:] = w_ref[right : right + count, :]
    tile = 256
    for n in range(FF // tile):
        cols = slice(n * tile, (n + 1) * tile)
        ups = slice(FF + n * tile, FF + (n + 1) * tile)
        gate = dot(x_ref[...], w_ref[:D, cols], NN)
        up = dot(x_ref[...], w_ref[:D, ups], NN)
        dh = dot(dym_ref[...], wd_ref[cols, :], NT)
        sig = jax.nn.sigmoid(gate)
        act = gate * sig
        slope = sig * (1.0 + gate * (1.0 - sig))
        h_ref[:, cols] = (act * up).astype(BF16)
        dz_ref[:, cols] = (dh * up * slope).astype(BF16)
        dz_ref[:, ups] = (dh * act).astype(BF16)
    ht_ref[...] = h_ref[...].T

    @pl.loop(0, D // tile)
    def _(i):
        rows = pl.ds(pl.multiple_of(i * tile, tile), tile)
        g_ref[rows, :] = dot(xt_ref[rows, :], dz_ref[...], NN).astype(BF16)

    for first, count, left, right in down_spans():
        part = dot(ht_ref[first : first + count, :], dym_ref[...], NN).astype(BF16)
        g_ref[left : left + count, :] = part[:, :WIDE]
        g_ref[right : right + count, :] = part[:, WIDE:]


def expert(count, x, xt, dy, weights):
    return pl.pallas_call(
        expert_kernel,
        out_shape=(
            jax.ShapeDtypeStruct((NBLK * BLK, WIDE), BF16),
            jax.ShapeDtypeStruct((ROWS, 2 * FF), BF16),
        ),
        in_specs=[pl.BlockSpec(memory_space=SMEM)] + [pl.BlockSpec(memory_space=VMEM)] * 4,
        out_specs=(pl.BlockSpec(memory_space=VMEM), pl.BlockSpec(memory_space=VMEM)),
        scratch_shapes=[
            VMEM((ROWS, D), BF16),
            VMEM((FF, D), BF16),
            VMEM((ROWS, FF), BF16),
            VMEM((FF, ROWS), BF16),
        ],
        compiler_params=params(48),
        name="expert",
    )(count, x, xt, dy, weights)


def row_grad_kernel(dz_ref, w_ref, out_ref):
    out_ref[...] = dot(dz_ref[...], w_ref[...], NT).astype(BF16)


def row_grad(dz, weights):
    tile = 256
    return pl.pallas_call(
        row_grad_kernel,
        grid=(D // tile,),
        out_shape=jax.ShapeDtypeStruct((ROWS, D), BF16),
        in_specs=[
            pl.BlockSpec((ROWS, 2 * FF), lambda i: (0, 0)),
            pl.BlockSpec((tile, WIDE), lambda i: (i, 0)),
        ],
        out_specs=pl.BlockSpec((ROWS, tile), lambda i: (0, i)),
        compiler_params=params(32),
        cost_estimate=pl.CostEstimate(flops=2 * ROWS * D * 2 * FF, bytes_accessed=8 << 20, transcendentals=0),
        name="row_grad",
    )(dz, weights)


def reduce_kernel(where_ref, place_ref, in_ref, o0, o1, o2, o3, acc_ref, line_ref):
    step = pl.program_id(0)

    @pl.when(step == 0)
    def _():
        acc_ref[...] = jnp.zeros_like(acc_ref)

    for k in range(4):
        e = place_ref[4 * step + k]
        acc_ref[e] += in_ref[k].astype(F32)

    @pl.when(step == pl.num_programs(0) - 1)
    def _():
        block = where_ref[0]
        group = where_ref[1]
        for shift, out in enumerate((o0, o1, o2, o3)):
            target = lax.rem(group + shift, 4)
            for j in range(PIECE):
                row = wire_row(block, PIECE * target + j)
                for e in range(4):
                    line_ref[e : e + 1, j * WIDE : (j + 1) * WIDE] = acc_ref[e, pl.ds(row, 1), :]
            out[...] = line_ref[...].astype(BF16)


def reduce(where, place, arrived):
    piece = jax.ShapeDtypeStruct((4, PIECE * WIDE), BF16)
    whole = pl.BlockSpec((4, PIECE * WIDE), lambda i: (0, 0))
    return pl.pallas_call(
        reduce_kernel,
        grid=(NBLK // 4,),
        out_shape=(piece,) * 4,
        in_specs=[pl.BlockSpec(memory_space=SMEM)] * 2 + [pl.BlockSpec((4, BLK, WIDE), lambda i: (i, 0, 0))],
        out_specs=(whole,) * 4,
        scratch_shapes=[VMEM((4, BLK, WIDE), F32), VMEM((4, PIECE * WIDE), F32)],
        compiler_params=params(32),
        name="reduce",
    )(where, place, arrived)


def sophia_kernel(where_ref, p0, p1, p2, p3, m_ref, c_ref, w_ref, mo_ref, co_ref, wo_ref, g_ref):
    group = where_ref[1]
    for shift, piece in enumerate((p0, p1, p2, p3)):
        source = lax.rem(group - shift + 4, 4)
        values = piece[...].astype(F32)
        for e in range(4):
            g_ref[pl.ds(4 * source + e, 1), :] = values[e : e + 1, :]
    grads = g_ref[...] * grad_scale
    momentum = beta_one * m_ref[...] + (1.0 - beta_one) * grads
    curvature = beta_two * c_ref[...] + (1.0 - beta_two) * grads * grads
    mo_ref[...] = momentum
    co_ref[...] = curvature
    wo_ref[...] = w_ref[...] - learn_rate * jnp.clip(momentum / (rho_scale * curvature), -1.0, 1.0)


def sophia(where, pieces, momentum, curvature, master):
    experts, length = master.shape
    tile = 4096
    state = pl.BlockSpec((experts, tile), lambda i: (0, i))
    return pl.pallas_call(
        sophia_kernel,
        grid=(length // tile,),
        out_shape=(jax.ShapeDtypeStruct(master.shape, F32),) * 3,
        in_specs=[pl.BlockSpec(memory_space=SMEM)] + [pl.BlockSpec((4, tile), lambda i: (0, i))] * 4 + [state] * 3,
        out_specs=(state,) * 3,
        scratch_shapes=[VMEM((experts, tile), F32)],
        compiler_params=params(32),
        name="sophia",
    )(where, *pieces, momentum, curvature, master)


def swap_y(pieces):
    out = [pieces[0]]
    for shift in (1, 2, 3):
        out.append(lax.ppermute(pieces[shift], "grp", [(g, (g + shift) % 4) for g in range(4)]))
    return out


def body(token_rows, cotangents, row_counts, old_place, new_place, momentum, curvature, master):
    group = lax.axis_index("grp")
    block = lax.axis_index("slot")
    where = jnp.stack([block, group]).astype(jnp.int32)
    outputs = []
    for step, place_map in ((0, old_place), (1, new_place)):
        place = lax.dynamic_index_in_dim(place_map, group, 1, keepdims=False)
        x, dy = token_rows[step, 0, 0], cotangents[step, 0, 0]
        count = row_counts[step].reshape(1)
        sends = [
            lax.dynamic_slice_in_dim(master, 4 * lax.rem(group + k, 4), 4, 0).astype(BF16)
            for k in range(4)
        ]
        outgoing = pack(where, place, swap_y(sends))
        weights = lax.all_to_all(outgoing, "slot", 0, 0, tiled=True).reshape(NBLK * BLK, WIDE)
        grads, dz = expert(count, x, x.T, dy, weights)
        arrived = lax.all_to_all(grads.reshape(NBLK, BLK, WIDE), "slot", 0, 0, tiled=True)
        outputs.append(row_grad(dz, weights))
        pieces = swap_y(reduce(where, place, arrived))
        momentum, curvature, master = sophia(where, pieces, momentum, curvature, master)
    return (jnp.stack(outputs)[:, None, None], momentum, curvature, master)


def solution(mesh):
    tokens = P(None, "slot", "grp", None, None)
    state = P(None, ("slot", "grp"))
    return jax.shard_map(
        body,
        mesh=mesh,
        in_specs=(tokens, tokens, P(None, "slot", "grp"), P(), P(), state, state, state),
        out_specs=(tokens, state, state, state),
        check_vma=False,
    )
```

```python
import jax
import jax.numpy as jnp
from jax import lax
from jax.experimental import pallas as pl
from jax.experimental.pallas import tpu as pltpu
from jax.sharding import PartitionSpec as P

D = 2048
FF = 512
ROWS = 384
WIDE = 1024
PIECE = 24
LANES = 128
LIMIT = 58
HALF = 1024

beta_one = 0.9
beta_two = 0.99
rho_scale = 2.0
learn_rate = 0.005
grad_scale = 0.25

F32 = jnp.float32
BF16 = jnp.bfloat16
VMEM = pltpu.VMEM
SMEM = pltpu.SMEM
in_smem = pl.BlockSpec(memory_space=SMEM)
in_hbm = pl.BlockSpec(memory_space=pl.ANY)

NT = (((1,), (1,)), ((), ()))
NN = (((1,), (0,)), ((), ()))


def params(limit_mb):
    return pltpu.CompilerParams(vmem_limit_bytes=limit_mb * 1024 * 1024)


def dot(a, b, dims):
    return lax.dot_general(a, b, dims, preferred_element_type=F32)


def to_rows(values, j, rows_ref):
    for c in range(WIDE // LANES):
        rows_ref[c, pl.ds(j, values.shape[0], PIECE), :] = values[:, c * LANES : (c + 1) * LANES]


def send_rows(ids_ref, rows_ref, bf_ref, out_ref, sem):
    for c in range(WIDE // LANES):
        for e in range(bf_ref.shape[0]):
            piece = rows_ref[c, e * PIECE : (e + 1) * PIECE, :]
            bf_ref[e, :, c * LANES : (c + 1) * LANES] = piece.astype(BF16)

    @pl.loop(0, out_ref.shape[0], unroll=4)
    def _(d):
        pltpu.make_async_copy(bf_ref.at[ids_ref[d]], out_ref.at[d], sem).start()


def row_scratch(experts):
    return VMEM((WIDE // LANES, experts * PIECE, LANES), F32)


def pack_kernel(ids_ref, w_ref, out_ref, w_buf, rows_ref, bf_ref, in_sem, sem):
    read = pltpu.make_async_copy(w_ref, w_buf, in_sem)
    read.start()
    read.wait()
    for j in range(PIECE):
        to_rows(w_buf[:, j * WIDE : (j + 1) * WIDE], j, rows_ref)
    send_rows(ids_ref, rows_ref, bf_ref, out_ref, sem)
    pltpu.make_async_copy(out_ref, out_ref, sem).wait()


def pack(ids, master):
    experts = master.shape[0]
    return pl.pallas_call(
        pack_kernel,
        out_shape=jax.ShapeDtypeStruct(ids.shape + (PIECE, WIDE), BF16),
        in_specs=[in_smem, in_hbm],
        out_specs=in_hbm,
        scratch_shapes=[
            VMEM(master.shape, F32),
            row_scratch(experts),
            VMEM((experts, PIECE, WIDE), BF16),
            pltpu.SemaphoreType.DMA,
            pltpu.SemaphoreType.DMA,
        ],
        compiler_params=params(LIMIT),
        name="pack",
    )(ids, master)


PARTS = 2
DEEP = D // PARTS
TILE = 256


def expert_kernel(x_hbm, xt_hbm, dy_hbm, w_ref, g_ref, dz_out, *scratch):
    x_ref, xt_ref, dy_ref, dz_ref, wgu_ref, wire_ref, wide_ref, wd_ref = scratch[:8]
    z_ref, dh_ref, h_ref, ht_ref, g_buf, in_sem, out_sem, dz_sem = scratch[8:]
    reads = []

    def read(source, target):
        reads.append(pltpu.make_async_copy(source, target, in_sem.at[len(reads)]))
        reads[-1].start()
        return reads[-1]

    down_in = read(w_ref.at[pl.ds(D, 2 * FF), :], wire_ref)
    dy_in = read(dy_hbm, dy_ref)
    x_in = read(x_hbm, x_ref)
    parts = []
    for k in range(PARTS):
        rows = pl.ds(k * DEEP, DEEP)
        parts.append(read(w_ref.at[rows, :], wgu_ref.at[rows, :]))
    xt_in = read(xt_hbm, xt_ref)

    down_in.wait()
    for t in range(2 * FF // TILE):
        down = slice(t * TILE // 2, (t + 1) * TILE // 2)
        for c in range(WIDE // LANES):
            wide_ref[c] = wire_ref[t * TILE : (t + 1) * TILE, c * LANES : (c + 1) * LANES].astype(F32)
            for half in range(2):
                first = half * HALF + c * LANES
                wd_ref[down, first : first + LANES] = wide_ref[c, pl.ds(half, TILE // 2, 2), :].astype(BF16)
    dy_in.wait()
    for n in range(FF // TILE):
        cols = slice(n * TILE, (n + 1) * TILE)
        dh_ref[:, cols] = dot(dy_ref[...], wd_ref[cols, :], NT)
    x_in.wait()
    for k in range(PARTS):
        parts[k].wait()
        rows = slice(k * DEEP, (k + 1) * DEEP)
        for n in range(2 * FF // TILE):
            cols = slice(n * TILE, (n + 1) * TILE)
            part = dot(x_ref[:, rows], wgu_ref[rows, cols], NN)
            z_ref[:, cols] = part if k == 0 else z_ref[:, cols] + part
    for n in range(FF // TILE):
        cols = slice(n * TILE, (n + 1) * TILE)
        ups = slice(FF + n * TILE, FF + (n + 1) * TILE)
        gate, up, dh = z_ref[:, cols], z_ref[:, ups], dh_ref[:, cols]
        sig = jax.nn.sigmoid(gate)
        act = gate * sig
        slope = sig * (1.0 + gate * (1.0 - sig))
        h_ref[:, cols] = (act * up).astype(BF16)
        dz_ref[:, cols] = (dh * up * slope).astype(BF16)
        dz_ref[:, ups] = (dh * act).astype(BF16)
    dz_copy = pltpu.make_async_copy(dz_ref, dz_out, dz_sem)
    dz_copy.start()
    ht_ref[...] = h_ref[...].T
    xt_in.wait()

    @pl.loop(0, D // TILE)
    def _(i):
        rows = pl.ds(pl.multiple_of(i * TILE, TILE), TILE)
        g_buf[rows, :] = dot(xt_ref[rows, :], dz_ref[...], NN).astype(BF16)
        pltpu.make_async_copy(g_buf.at[rows, :], g_ref.at[rows, :], out_sem).start()

    @pl.loop(0, 2 * FF // TILE)
    def _(i):
        rows = pl.ds(pl.multiple_of(i * (TILE // 2), TILE // 2), TILE // 2)
        part = dot(ht_ref[rows, :], dy_ref[...], NN)
        wire = pl.ds(pl.multiple_of(D + i * TILE, TILE), TILE)
        for c in range(WIDE // LANES):
            for half in range(2):
                first = half * HALF + c * LANES
                wide_ref[c, pl.ds(half, TILE // 2, 2), :] = part[:, first : first + LANES]
            g_buf[wire, c * LANES : (c + 1) * LANES] = wide_ref[c].astype(BF16)
        pltpu.make_async_copy(g_buf.at[wire, :], g_ref.at[wire, :], out_sem).start()

    pltpu.make_async_copy(g_buf, g_ref, out_sem).wait()
    dz_copy.wait()


def expert(x, xt, dy, weights):
    return pl.pallas_call(
        expert_kernel,
        out_shape=(
            jax.ShapeDtypeStruct(weights.shape, BF16),
            jax.ShapeDtypeStruct((ROWS, 2 * FF), BF16),
        ),
        in_specs=[in_hbm] * 4,
        out_specs=(in_hbm, in_hbm),
        scratch_shapes=[
            VMEM((ROWS, D), BF16),
            VMEM((D, ROWS), BF16),
            VMEM((ROWS, D), BF16),
            VMEM((ROWS, 2 * FF), BF16),
            VMEM((D, 2 * FF), BF16),
            VMEM((2 * FF, WIDE), BF16),
            VMEM((WIDE // LANES, TILE, LANES), F32),
            VMEM((FF, D), BF16),
            VMEM((ROWS, 2 * FF), F32),
            VMEM((ROWS, FF), F32),
            VMEM((ROWS, FF), BF16),
            VMEM((FF, ROWS), BF16),
            VMEM(weights.shape, BF16),
            pltpu.SemaphoreType.DMA((PARTS + 4,)),
            pltpu.SemaphoreType.DMA,
            pltpu.SemaphoreType.DMA,
        ],
        compiler_params=params(LIMIT),
        name="expert",
    )(x, xt, dy, weights)


def row_grad_kernel(dz_ref, w_ref, out_ref):
    out_ref[...] = dot(dz_ref[...], w_ref[...], NT).astype(BF16)


def row_grad(dz, weights):
    return pl.pallas_call(
        row_grad_kernel,
        grid=(D // TILE,),
        out_shape=jax.ShapeDtypeStruct((ROWS, D), BF16),
        in_specs=[
            pl.BlockSpec((ROWS, 2 * FF), lambda i: (0, 0)),
            pl.BlockSpec((TILE, WIDE), lambda i: (i, 0)),
        ],
        out_specs=pl.BlockSpec((ROWS, TILE), lambda i: (0, i)),
        compiler_params=params(32),
        cost_estimate=pl.CostEstimate(flops=2 * ROWS * D * 2 * FF, bytes_accessed=8 << 20, transcendentals=0),
        name="row_grad",
    )(dz, weights)


def sophia(grads, momentum, curvature, master):
    momentum = beta_one * momentum + (1.0 - beta_one) * grads
    curvature = beta_two * curvature + (1.0 - beta_two) * grads * grads
    master = master - learn_rate * jnp.clip(momentum / (rho_scale * curvature), -1.0, 1.0)
    return momentum, curvature, master


GROUP = 16


def add_slots(ids_ref, in_ref, buf_ref, acc_ref, sems):
    def read(k):
        part = pl.ds(k * GROUP, GROUP)
        return pltpu.make_async_copy(in_ref.at[part], buf_ref.at[part], sems.at[k])

    groups = buf_ref.shape[0] // GROUP
    for k in range(groups):
        read(k).start()
    acc_ref[...] = jnp.zeros_like(acc_ref)

    @pl.loop(0, groups)
    def _(k):
        read(k).wait()

        @pl.loop(0, GROUP, unroll=4)
        def _(i):
            d = k * GROUP + i
            rows = pl.ds(pl.multiple_of(ids_ref[d] * PIECE, 8), PIECE)
            for c in range(WIDE // LANES):
                acc_ref[c, rows, :] += buf_ref[d, :, c * LANES : (c + 1) * LANES].astype(F32)


def from_rows(acc_ref, j, experts):
    parts = [acc_ref[c, pl.ds(j, experts, PIECE), :] for c in range(WIDE // LANES)]
    return jnp.concatenate(parts, axis=1) * grad_scale


def first_update_kernel(ids_ref, next_ref, in_ref, m_ref, c_ref, w_ref, g_ref, out_ref, *scratch):
    buf_ref, acc_ref, rows_ref, bf_ref, m_buf, c_buf, w_buf, g_buf, sems, state_sem, out_sem, g_sem = scratch
    state = [
        pltpu.make_async_copy(a, b, state_sem.at[i])
        for i, (a, b) in enumerate(((m_ref, m_buf), (c_ref, c_buf), (w_ref, w_buf)))
    ]
    for copy in state:
        copy.start()
    add_slots(ids_ref, in_ref, buf_ref, acc_ref, sems)
    for copy in state:
        copy.wait()
    for j in range(PIECE):
        cols = slice(j * WIDE, (j + 1) * WIDE)
        grads = from_rows(acc_ref, j, m_buf.shape[0])
        g_buf[:, cols] = grads
        to_rows(sophia(grads, m_buf[:, cols], c_buf[:, cols], w_buf[:, cols])[2], j, rows_ref)
    send_rows(next_ref, rows_ref, bf_ref, out_ref, out_sem)
    g_copy = pltpu.make_async_copy(g_buf, g_ref, g_sem)
    g_copy.start()
    pltpu.make_async_copy(out_ref, out_ref, out_sem).wait()
    g_copy.wait()


def first_update(ids, next_ids, arrived, momentum, curvature, master):
    experts = master.shape[0]
    dma = pltpu.SemaphoreType.DMA
    return pl.pallas_call(
        first_update_kernel,
        out_shape=(jax.ShapeDtypeStruct(master.shape, F32), jax.ShapeDtypeStruct(arrived.shape, BF16)),
        in_specs=[in_smem] * 2 + [in_hbm] * 4,
        out_specs=(in_hbm,) * 2,
        scratch_shapes=[
            VMEM(arrived.shape, BF16),
            row_scratch(experts),
            row_scratch(experts),
            VMEM((experts, PIECE, WIDE), BF16),
        ]
        + [VMEM(master.shape, F32)] * 4
        + [dma((arrived.shape[0] // GROUP,)), dma((3,)), dma, dma],
        compiler_params=params(LIMIT),
        name="first_update",
    )(ids, next_ids, arrived, momentum, curvature, master)


def last_update_kernel(ids_ref, in_ref, m_ref, c_ref, w_ref, mo_ref, co_ref, wo_ref, *scratch):
    buf_ref, acc_ref, m_buf, c_buf, w_buf, sems, state_sem, out_sem = scratch
    state = [
        pltpu.make_async_copy(a, b, state_sem.at[i])
        for i, (a, b) in enumerate(((m_ref, m_buf), (c_ref, c_buf), (w_ref, w_buf)))
    ]
    for copy in state:
        copy.start()
    add_slots(ids_ref, in_ref, buf_ref, acc_ref, sems)
    for copy in state:
        copy.wait()
    for j in range(PIECE):
        cols = slice(j * WIDE, (j + 1) * WIDE)
        grads = from_rows(acc_ref, j, m_buf.shape[0])
        values = sophia(grads, m_buf[:, cols], c_buf[:, cols], w_buf[:, cols])
        for i, (buf, out) in enumerate(((m_buf, mo_ref), (c_buf, co_ref), (w_buf, wo_ref))):
            buf[:, cols] = values[i]
            pltpu.make_async_copy(buf.at[:, cols], out.at[:, cols], out_sem.at[i]).start()
    for i, (buf, out) in enumerate(((m_buf, mo_ref), (c_buf, co_ref), (w_buf, wo_ref))):
        pltpu.make_async_copy(buf, out, out_sem.at[i]).wait()


def last_update(ids, arrived, momentum, curvature, master):
    experts = master.shape[0]
    dma = pltpu.SemaphoreType.DMA
    return pl.pallas_call(
        last_update_kernel,
        out_shape=(jax.ShapeDtypeStruct(master.shape, F32),) * 3,
        in_specs=[in_smem] + [in_hbm] * 4,
        out_specs=(in_hbm,) * 3,
        scratch_shapes=[VMEM(arrived.shape, BF16), row_scratch(experts)]
        + [VMEM(master.shape, F32)] * 3
        + [dma((arrived.shape[0] // GROUP,)), dma((3,)), dma((3,))],
        compiler_params=params(LIMIT),
        name="last_update",
    )(ids, arrived, momentum, curvature, master)


def exchange(blocks):
    return lax.all_to_all(blocks, ("slot", "grp"), 0, 0, tiled=True)


def body(token_rows, cotangents, row_counts, old_place, new_place, momentum, curvature, master):
    groups = lax.axis_size("grp")
    experts = master.shape[0]
    owners = (jnp.arange(groups, dtype=jnp.int32) * (experts // groups))[None, :]
    old_ids = (old_place + owners).reshape(-1)
    new_ids = (new_place + owners).reshape(-1)

    def slots(step, outgoing):
        arrived = exchange(outgoing)
        weights = arrived.reshape(-1, WIDE)
        live = jnp.arange(ROWS, dtype=jnp.int32)[:, None] < row_counts[step, 0, 0]
        x = token_rows[step, 0, 0]
        dy = jnp.where(live, cotangents[step, 0, 0], jnp.zeros((), BF16))
        grads, dz = expert(x, x.T, dy, weights)
        return exchange(grads.reshape(arrived.shape)), row_grad(dz, weights)

    arrived, first_rows = slots(0, pack(old_ids, master))
    grads, outgoing = first_update(old_ids, new_ids, arrived, momentum, curvature, master)
    state = sophia(grads, momentum, curvature, master)
    arrived, last_rows = slots(1, outgoing)
    state = last_update(new_ids, arrived, *state)
    return (jnp.stack([first_rows, last_rows])[:, None, None], *state)


def solution(mesh):
    tokens = P(None, "slot", "grp", None, None)
    state = P(None, ("slot", "grp"))
    return jax.shard_map(
        body,
        mesh=mesh,
        in_specs=(tokens, tokens, P(None, "slot", "grp"), P(), P(), state, state, state),
        out_specs=(tokens, state, state, state),
        check_vma=False,
    )
```

```python
import jax
import jax.numpy as jnp
from jax import lax
from jax.experimental import pallas as pl
from jax.experimental.pallas import tpu as pltpu
from jax.sharding import PartitionSpec as P

D = 2048
FF = 512
ROWS = 384
WIDE = 1024
PIECE = 24
LANES = 128
EXPERTS = 16
LIMIT = 58
HALF = 1024

beta_one = 0.9
beta_two = 0.99
rho_scale = 2.0
learn_rate = 0.005
grad_scale = 0.25

F32 = jnp.float32
BF16 = jnp.bfloat16
VMEM = pltpu.VMEM
SMEM = pltpu.SMEM
in_smem = pl.BlockSpec(memory_space=SMEM)
in_hbm = pl.BlockSpec(memory_space=pl.ANY)

NT = (((1,), (1,)), ((), ()))
NN = (((1,), (0,)), ((), ()))
TN = (((0,), (0,)), ((), ()))


def params(limit_mb):
    return pltpu.CompilerParams(vmem_limit_bytes=limit_mb * 1024 * 1024)


def dot(a, b, dims):
    return lax.dot_general(a, b, dims, preferred_element_type=F32)


def expert_of(place_ref, d):
    groups = place_ref.shape[0]
    group = lax.rem(d, groups)
    return place_ref[group, lax.div(d, groups)] + group * (EXPERTS // groups)


def to_rows(values, j, rows_ref):
    for c in range(WIDE // LANES):
        rows_ref[c, pl.ds(j, values.shape[0], PIECE), :] = values[:, c * LANES : (c + 1) * LANES]


def send_rows(place_ref, bf_ref, out_ref, sem):
    @pl.loop(0, out_ref.shape[0], unroll=4)
    def _(d):
        pltpu.make_async_copy(bf_ref.at[expert_of(place_ref, d)], out_ref.at[d], sem).start()


ROW_STATE = (WIDE // LANES, EXPERTS * PIECE, LANES)


def pack_kernel(place_ref, w_ref, out_ref, w_buf, rows_ref, bf_ref, in_sem, sem):
    read = pltpu.make_async_copy(w_ref, w_buf, in_sem)
    read.start()
    read.wait()
    for j in range(PIECE):
        to_rows(w_buf[:, j * WIDE : (j + 1) * WIDE], j, rows_ref)
    for c in range(WIDE // LANES):
        for e in range(EXPERTS):
            piece = rows_ref[c, e * PIECE : (e + 1) * PIECE, :]
            bf_ref[e, :, c * LANES : (c + 1) * LANES] = piece.astype(BF16)
    send_rows(place_ref, bf_ref, out_ref, sem)
    pltpu.make_async_copy(out_ref, out_ref, sem).wait()


def pack(place, master):
    return pl.pallas_call(
        pack_kernel,
        out_shape=jax.ShapeDtypeStruct((place.size, PIECE, WIDE), BF16),
        in_specs=[in_smem, in_hbm],
        out_specs=in_hbm,
        scratch_shapes=[
            VMEM(master.shape, F32),
            VMEM(ROW_STATE, F32),
            VMEM((EXPERTS, PIECE, WIDE), BF16),
            pltpu.SemaphoreType.DMA,
            pltpu.SemaphoreType.DMA,
        ],
        compiler_params=params(LIMIT),
        name="pack",
    )(place, master)


def rows_kernel(in_ref, out_ref):
    for j in range(PIECE):
        to_rows(in_ref[:, j * WIDE : (j + 1) * WIDE], j, out_ref)


def rows_of(values):
    return pl.pallas_call(
        rows_kernel,
        out_shape=jax.ShapeDtypeStruct(ROW_STATE, F32),
        compiler_params=params(LIMIT),
        cost_estimate=pl.CostEstimate(flops=values.size, bytes_accessed=8 * values.size, transcendentals=0),
        name="rows_of",
    )(values)


PARTS = 2
DEEP = D // PARTS
TILE = 256


def expert_kernel(x_hbm, dy_hbm, w_ref, g_ref, dz_out, *scratch):
    x_ref, dy_ref, dz_ref, wgu_ref, wire_ref, wide_ref, wd_ref = scratch[:7]
    z_ref, dh_ref, h_ref, ht_ref, g_buf, in_sem, out_sem, dz_sem = scratch[7:]
    reads = []

    def read(source, target):
        reads.append(pltpu.make_async_copy(source, target, in_sem.at[len(reads)]))
        reads[-1].start()
        return reads[-1]

    down_in = read(w_ref.at[pl.ds(D, 2 * FF), :], wire_ref)
    dy_in = read(dy_hbm, dy_ref)
    x_in = read(x_hbm, x_ref)
    parts = []
    for k in range(PARTS):
        rows = pl.ds(k * DEEP, DEEP)
        parts.append(read(w_ref.at[rows, :], wgu_ref.at[rows, :]))

    down_in.wait()
    for t in range(2 * FF // TILE):
        down = slice(t * TILE // 2, (t + 1) * TILE // 2)
        for c in range(WIDE // LANES):
            wide_ref[c] = wire_ref[t * TILE : (t + 1) * TILE, c * LANES : (c + 1) * LANES].astype(F32)
            for half in range(2):
                first = half * HALF + c * LANES
                wd_ref[down, first : first + LANES] = wide_ref[c, pl.ds(half, TILE // 2, 2), :].astype(BF16)
    dy_in.wait()
    for n in range(FF // TILE):
        cols = slice(n * TILE, (n + 1) * TILE)
        dh_ref[:, cols] = dot(dy_ref[...], wd_ref[cols, :], NT)
    x_in.wait()
    for k in range(PARTS):
        parts[k].wait()
        rows = slice(k * DEEP, (k + 1) * DEEP)
        for n in range(FF // TILE):
            cols = slice(n * TILE, (n + 1) * TILE)
            ups = slice(FF + n * TILE, FF + (n + 1) * TILE)
            gate = dot(x_ref[:, rows], wgu_ref[rows, cols], NN)
            up = dot(x_ref[:, rows], wgu_ref[rows, ups], NN)
            if k > 0:
                gate, up = gate + z_ref[:, cols], up + z_ref[:, ups]
            if k < PARTS - 1:
                z_ref[:, cols], z_ref[:, ups] = gate, up
                continue
            dh = dh_ref[:, cols]
            sig = jax.nn.sigmoid(gate)
            act = gate * sig
            slope = sig * (1.0 + gate * (1.0 - sig))
            h_ref[:, cols] = (act * up).astype(BF16)
            dz_ref[:, cols] = (dh * up * slope).astype(BF16)
            dz_ref[:, ups] = (dh * act).astype(BF16)
    dz_copy = pltpu.make_async_copy(dz_ref, dz_out, dz_sem)
    dz_copy.start()
    ht_ref[...] = h_ref[...].T

    for i in range(D // TILE):
        rows = slice(i * TILE, (i + 1) * TILE)
        g_buf[rows, :] = dot(x_ref[:, rows], dz_ref[...], TN).astype(BF16)
        pltpu.make_async_copy(g_buf.at[pl.ds(i * TILE, TILE), :], g_ref.at[pl.ds(i * TILE, TILE), :], out_sem).start()

    @pl.loop(0, 2 * FF // TILE, unroll=True)
    def _(i):
        rows = pl.ds(pl.multiple_of(i * (TILE // 2), TILE // 2), TILE // 2)
        part = dot(ht_ref[rows, :], dy_ref[...], NN)
        wire = pl.ds(pl.multiple_of(D + i * TILE, TILE), TILE)
        for c in range(WIDE // LANES):
            for half in range(2):
                first = half * HALF + c * LANES
                wide_ref[c, pl.ds(half, TILE // 2, 2), :] = part[:, first : first + LANES]
            g_buf[wire, c * LANES : (c + 1) * LANES] = wide_ref[c].astype(BF16)
        pltpu.make_async_copy(g_buf.at[wire, :], g_ref.at[wire, :], out_sem).start()

    pltpu.make_async_copy(g_buf, g_ref, out_sem).wait()
    dz_copy.wait()


def expert(x, dy, weights):
    return pl.pallas_call(
        expert_kernel,
        out_shape=(
            jax.ShapeDtypeStruct(weights.shape, BF16),
            jax.ShapeDtypeStruct((ROWS, 2 * FF), BF16),
        ),
        in_specs=[in_hbm] * 3,
        out_specs=(in_hbm, in_hbm),
        scratch_shapes=[
            VMEM((ROWS, D), BF16),
            VMEM((ROWS, D), BF16),
            VMEM((ROWS, 2 * FF), BF16),
            VMEM((D, 2 * FF), BF16),
            VMEM((2 * FF, WIDE), BF16),
            VMEM((WIDE // LANES, TILE, LANES), F32),
            VMEM((FF, D), BF16),
            VMEM((ROWS, 2 * FF), F32),
            VMEM((ROWS, FF), F32),
            VMEM((ROWS, FF), BF16),
            VMEM((FF, ROWS), BF16),
            VMEM(weights.shape, BF16),
            pltpu.SemaphoreType.DMA((PARTS + 3,)),
            pltpu.SemaphoreType.DMA,
            pltpu.SemaphoreType.DMA,
        ],
        compiler_params=params(LIMIT),
        name="expert",
    )(x, dy, weights)


def row_grad_kernel(dz_ref, w_ref, out_ref):
    out_ref[...] = dot(dz_ref[...], w_ref[...], NT).astype(BF16)


def row_grad(dz, weights):
    return pl.pallas_call(
        row_grad_kernel,
        grid=(D // TILE,),
        out_shape=jax.ShapeDtypeStruct((ROWS, D), BF16),
        in_specs=[
            pl.BlockSpec((ROWS, 2 * FF), lambda i: (0, 0)),
            pl.BlockSpec((TILE, WIDE), lambda i: (i, 0)),
        ],
        out_specs=pl.BlockSpec((ROWS, TILE), lambda i: (0, i)),
        compiler_params=params(32),
        cost_estimate=pl.CostEstimate(flops=2 * ROWS * D * 2 * FF, bytes_accessed=8 << 20, transcendentals=0),
        name="row_grad",
    )(dz, weights)


def sophia(grads, momentum, curvature, master):
    momentum = beta_one * momentum + (1.0 - beta_one) * grads
    curvature = beta_two * curvature + (1.0 - beta_two) * grads * grads
    master = master - learn_rate * jnp.clip(momentum / (rho_scale * curvature), -1.0, 1.0)
    return momentum, curvature, master


GROUP = 16
UNROLL = 2


def add_slots(place_ref, in_ref, buf_ref, acc_ref, sems):
    def read(k):
        part = pl.ds(k * GROUP, GROUP)
        return pltpu.make_async_copy(in_ref.at[part], buf_ref.at[part], sems.at[k])

    groups = buf_ref.shape[0] // GROUP
    for k in range(groups):
        read(k).start()
    for acc in acc_ref:
        acc[...] = jnp.zeros_like(acc)

    @pl.loop(0, groups)
    def _(k):
        read(k).wait()

        @pl.loop(0, GROUP, step=2 * UNROLL)
        def _(i):
            for u in range(2 * UNROLL):
                d = k * GROUP + i + u
                acc = acc_ref[u % 2]
                rows = pl.ds(pl.multiple_of(expert_of(place_ref, d) * PIECE, 8), PIECE)
                for c in range(WIDE // LANES):
                    acc[c, rows, :] += buf_ref[d, :, c * LANES : (c + 1) * LANES].astype(F32)


def from_rows(acc_ref, j):
    parts = [acc_ref[c, pl.ds(j, EXPERTS, PIECE), :] for c in range(WIDE // LANES)]
    return jnp.concatenate(parts, axis=1)


def first_update_kernel(place_ref, next_ref, in_ref, m_ref, c_ref, w_ref, g_ref, out_ref, *scratch):
    buf_ref, even_ref, odd_ref, bf_ref, m_buf, c_buf, w_buf, sems, state_sem, out_sem, g_sem = scratch
    state = [
        pltpu.make_async_copy(a, b, state_sem.at[i])
        for i, (a, b) in enumerate(((m_ref, m_buf), (c_ref, c_buf), (w_ref, w_buf)))
    ]
    for copy in state:
        copy.start()
    add_slots(place_ref, in_ref, buf_ref, (even_ref, odd_ref), sems)
    for copy in state:
        copy.wait()

    @pl.loop(0, EXPERTS)
    def _(e):
        rows = pl.ds(pl.multiple_of(e * PIECE, 8), PIECE)
        for c in range(WIDE // LANES):
            grads = (even_ref[c, rows, :] + odd_ref[c, rows, :]) * grad_scale
            even_ref[c, rows, :] = grads
            master = sophia(grads, m_buf[c, rows, :], c_buf[c, rows, :], w_buf[c, rows, :])[2]
            bf_ref[e, :, c * LANES : (c + 1) * LANES] = master.astype(BF16)

    send_rows(next_ref, bf_ref, out_ref, out_sem)
    g_copy = pltpu.make_async_copy(even_ref, g_ref, g_sem)
    g_copy.start()
    pltpu.make_async_copy(out_ref, out_ref, out_sem).wait()
    g_copy.wait()


def first_update(place, next_place, arrived, momentum, curvature, master):
    dma = pltpu.SemaphoreType.DMA
    return pl.pallas_call(
        first_update_kernel,
        out_shape=(jax.ShapeDtypeStruct(ROW_STATE, F32), jax.ShapeDtypeStruct(arrived.shape, BF16)),
        in_specs=[in_smem] * 2 + [in_hbm] * 4,
        out_specs=(in_hbm,) * 2,
        scratch_shapes=[VMEM(arrived.shape, BF16)]
        + [VMEM(ROW_STATE, F32)] * 2
        + [VMEM((EXPERTS, PIECE, WIDE), BF16)]
        + [VMEM(ROW_STATE, F32)] * 3
        + [dma((arrived.shape[0] // GROUP,)), dma((3,)), dma, dma],
        compiler_params=params(LIMIT),
        name="first_update",
    )(place, next_place, arrived, momentum, curvature, master)


def first_state_kernel(g_ref, m_ref, c_ref, w_ref, mo_ref, co_ref, wo_ref):
    for j in range(PIECE):
        cols = slice(j * WIDE, (j + 1) * WIDE)
        values = sophia(from_rows(g_ref, j), m_ref[:, cols], c_ref[:, cols], w_ref[:, cols])
        mo_ref[:, cols], co_ref[:, cols], wo_ref[:, cols] = values


def first_state(grads, momentum, curvature, master):
    return pl.pallas_call(
        first_state_kernel,
        out_shape=(jax.ShapeDtypeStruct(master.shape, F32),) * 3,
        compiler_params=params(LIMIT),
        cost_estimate=pl.CostEstimate(flops=9 * master.size, bytes_accessed=28 * master.size, transcendentals=0),
        name="first_state",
    )(grads, momentum, curvature, master)


def last_update_kernel(place_ref, in_ref, m_ref, c_ref, w_ref, mo_ref, co_ref, wo_ref, *scratch):
    buf_ref, even_ref, odd_ref, m_buf, c_buf, w_buf, sems, state_sem, out_sem = scratch
    state = [
        pltpu.make_async_copy(a, b, state_sem.at[i])
        for i, (a, b) in enumerate(((m_ref, m_buf), (c_ref, c_buf), (w_ref, w_buf)))
    ]
    for copy in state:
        copy.start()
    add_slots(place_ref, in_ref, buf_ref, (even_ref, odd_ref), sems)
    for copy in state:
        copy.wait()
    for j in range(PIECE):
        cols = slice(j * WIDE, (j + 1) * WIDE)
        grads = (from_rows(even_ref, j) + from_rows(odd_ref, j)) * grad_scale
        values = sophia(grads, m_buf[:, cols], c_buf[:, cols], w_buf[:, cols])
        for i, (buf, out) in enumerate(((m_buf, mo_ref), (c_buf, co_ref), (w_buf, wo_ref))):
            buf[:, cols] = values[i]
            pltpu.make_async_copy(buf.at[:, cols], out.at[:, cols], out_sem.at[i]).start()
    for i, (buf, out) in enumerate(((m_buf, mo_ref), (c_buf, co_ref), (w_buf, wo_ref))):
        pltpu.make_async_copy(buf, out, out_sem.at[i]).wait()


def last_update(place, arrived, momentum, curvature, master):
    dma = pltpu.SemaphoreType.DMA
    return pl.pallas_call(
        last_update_kernel,
        out_shape=(jax.ShapeDtypeStruct(master.shape, F32),) * 3,
        in_specs=[in_smem] + [in_hbm] * 4,
        out_specs=(in_hbm,) * 3,
        scratch_shapes=[VMEM(arrived.shape, BF16)]
        + [VMEM(ROW_STATE, F32)] * 2
        + [VMEM(master.shape, F32)] * 3
        + [dma((arrived.shape[0] // GROUP,)), dma((3,)), dma((3,))],
        compiler_params=params(LIMIT),
        name="last_update",
    )(place, arrived, momentum, curvature, master)


def exchange(blocks):
    return lax.all_to_all(blocks, ("slot", "grp"), 0, 0, tiled=True)


def body(token_rows, cotangents, row_counts, old_place, new_place, momentum, curvature, master):
    old_place, new_place = old_place.T, new_place.T

    def slots(step, outgoing):
        arrived = exchange(outgoing)
        weights = arrived.reshape(-1, WIDE)
        live = jnp.arange(ROWS, dtype=jnp.int32)[:, None] < row_counts[step, 0, 0]
        dy = jnp.where(live, cotangents[step, 0, 0], jnp.zeros((), BF16))
        grads, dz = expert(token_rows[step, 0, 0], dy, weights)
        return exchange(grads.reshape(arrived.shape)), row_grad(dz, weights)

    arrived, first_rows = slots(0, pack(old_place, master))
    state = [rows_of(v) for v in (momentum, curvature, master)]
    grads, outgoing = first_update(old_place, new_place, arrived, *state)
    arrived, last_rows = slots(1, outgoing)
    state = first_state(grads, momentum, curvature, master)
    state = last_update(new_place, arrived, *state)
    return (jnp.stack([first_rows, last_rows])[:, None, None], *state)


def solution(mesh):
    tokens = P(None, "slot", "grp", None, None)
    state = P(None, ("slot", "grp"))
    return jax.shard_map(
        body,
        mesh=mesh,
        in_specs=(tokens, tokens, P(None, "slot", "grp"), P(), P(), state, state, state),
        out_specs=(tokens, state, state, state),
        check_vma=False,
    )
```

```python
import functools

import jax
import jax.numpy as jnp
from jax import lax
from jax.experimental import pallas as pl
from jax.experimental.pallas import tpu as pltpu
from jax.sharding import PartitionSpec as P

D = 2048
FF = 512
ROWS = 384
WIDE = 1024
PIECE = 24
LANES = 128
EXPERTS = 16
LIMIT = 58
HALF = 1024

beta_one = 0.9
beta_two = 0.99
rho_scale = 2.0
learn_rate = 0.005
grad_scale = 0.25

F32 = jnp.float32
BF16 = jnp.bfloat16
VMEM = pltpu.VMEM
SMEM = pltpu.SMEM
in_hbm = pl.BlockSpec(memory_space=pl.ANY)

NT = (((1,), (1,)), ((), ()))
NN = (((1,), (0,)), ((), ()))
TN = (((0,), (0,)), ((), ()))


def params(limit_mb):
    return pltpu.CompilerParams(vmem_limit_bytes=limit_mb * 1024 * 1024)


def dot(a, b, dims):
    return lax.dot_general(a, b, dims, preferred_element_type=F32)


def expert_of(place_ref, d):
    groups = place_ref.shape[0]
    group = lax.rem(d, groups)
    return place_ref[group, lax.div(d, groups)] + group * (EXPERTS // groups)


def to_rows(values, j, rows_ref):
    for c in range(WIDE // LANES):
        rows_ref[c, pl.ds(j, values.shape[0], PIECE), :] = values[:, c * LANES : (c + 1) * LANES]


BATCH = 4
GROUP = 8


def round_rows(rows_ref, bf_ref):
    for c in range(WIDE // LANES):
        for e in range(EXPERTS):
            piece = rows_ref[c, e * PIECE : (e + 1) * PIECE, :]
            bf_ref[e, :, c * LANES : (c + 1) * LANES] = piece.astype(BF16)


def send_rows(place_ref, bf_ref, all_ref, out_ref, sem):
    @pl.loop(0, all_ref.shape[0] // GROUP)
    def _(k):
        @pl.loop(0, GROUP, unroll=8)
        def _(i):
            d = k * GROUP + i
            all_ref[d] = bf_ref[expert_of(place_ref, d)]

        part = pl.ds(k * GROUP, GROUP)
        pltpu.make_async_copy(all_ref.at[part], out_ref.at[part], sem).start()


ROW_STATE = (WIDE // LANES, EXPERTS * PIECE, LANES)


def pack_kernel(place_hbm, w_ref, out_ref, w_buf, rows_ref, bf_ref, all_ref, place_ref, in_sem, sem, place_sem):
    reads = []
    for k in range(PIECE // BATCH):
        cols = pl.ds(k * BATCH * WIDE, BATCH * WIDE)
        reads.append(pltpu.make_async_copy(w_ref.at[:, cols], w_buf.at[:, cols], in_sem.at[k]))
        reads[k].start()
    place_in = pltpu.make_async_copy(place_hbm, place_ref, place_sem)
    place_in.start()
    for j in range(PIECE):
        if j % BATCH == 0:
            reads[j // BATCH].wait()
        to_rows(w_buf[:, j * WIDE : (j + 1) * WIDE], j, rows_ref)
    round_rows(rows_ref, bf_ref)
    place_in.wait()
    send_rows(place_ref, bf_ref, all_ref, out_ref, sem)
    pltpu.make_async_copy(all_ref, out_ref, sem).wait()


def pack(place, master):
    return pl.pallas_call(
        pack_kernel,
        out_shape=jax.ShapeDtypeStruct((place.size, PIECE, WIDE), BF16),
        in_specs=[in_hbm] * 2,
        out_specs=in_hbm,
        scratch_shapes=[
            VMEM(master.shape, F32),
            VMEM(ROW_STATE, F32),
            VMEM((EXPERTS, PIECE, WIDE), BF16),
            VMEM((place.size, PIECE, WIDE), BF16),
            SMEM(place.shape, jnp.int32),
            pltpu.SemaphoreType.DMA((PIECE // BATCH,)),
            pltpu.SemaphoreType.DMA,
            pltpu.SemaphoreType.DMA,
        ],
        compiler_params=params(LIMIT),
        name="pack",
    )(place, master)


PARTS = 2
DEEP = D // PARTS
TILE = 256


def expert_kernel(step, count_hbm, x_hbm, dy_hbm, w_ref, g_ref, dz_out, *scratch):
    x_ref, dy_ref, dz_ref, wgu_ref, wire_ref, wide_ref, wd_ref = scratch[:7]
    z_ref, dh_ref, h_ref, ht_ref, g_buf, count_ref, in_sem, out_sem, dz_sem = scratch[7:]
    reads = []

    def read(source, target):
        reads.append(pltpu.make_async_copy(source, target, in_sem.at[len(reads)]))
        reads[-1].start()
        return reads[-1]

    down_in = read(w_ref.at[pl.ds(D, 2 * FF), :], wire_ref)
    dy_in = read(dy_hbm.at[step], dy_ref)
    x_in = read(x_hbm.at[step], x_ref)
    parts = []
    for k in range(PARTS):
        rows = pl.ds(k * DEEP, DEEP)
        parts.append(read(w_ref.at[rows, :], wgu_ref.at[rows, :]))

    count_in = read(count_hbm, count_ref)

    down_in.wait()
    for t in range(2 * FF // TILE):
        down = slice(t * TILE // 2, (t + 1) * TILE // 2)
        for c in range(WIDE // LANES):
            wide_ref[c] = wire_ref[t * TILE : (t + 1) * TILE, c * LANES : (c + 1) * LANES].astype(F32)
            for half in range(2):
                first = half * HALF + c * LANES
                wd_ref[down, first : first + LANES] = wide_ref[c, pl.ds(half, TILE // 2, 2), :].astype(BF16)
    dy_in.wait()
    for n in range(FF // TILE):
        cols = slice(n * TILE, (n + 1) * TILE)
        dh_ref[:, cols] = dot(dy_ref[...], wd_ref[cols, :], NT)
    count_in.wait()
    live = lax.broadcasted_iota(jnp.int32, (ROWS, TILE), 0) < count_ref[step]
    x_in.wait()
    for k in range(PARTS):
        parts[k].wait()
        rows = slice(k * DEEP, (k + 1) * DEEP)
        for n in range(FF // TILE):
            cols = slice(n * TILE, (n + 1) * TILE)
            ups = slice(FF + n * TILE, FF + (n + 1) * TILE)
            gate = dot(x_ref[:, rows], wgu_ref[rows, cols], NN)
            up = dot(x_ref[:, rows], wgu_ref[rows, ups], NN)
            if k > 0:
                gate, up = gate + z_ref[:, cols], up + z_ref[:, ups]
            if k < PARTS - 1:
                z_ref[:, cols], z_ref[:, ups] = gate, up
                continue
            dh = jnp.where(live, dh_ref[:, cols], 0.0)
            sig = jax.nn.sigmoid(gate)
            act = gate * sig
            slope = sig * (1.0 + gate * (1.0 - sig))
            h_ref[:, cols] = jnp.where(live, act * up, 0.0).astype(BF16)
            dz_ref[:, cols] = (dh * up * slope).astype(BF16)
            dz_ref[:, ups] = (dh * act).astype(BF16)
    dz_copy = pltpu.make_async_copy(dz_ref, dz_out, dz_sem)
    dz_copy.start()
    ht_ref[...] = h_ref[...].T

    for i in range(D // TILE):
        rows = slice(i * TILE, (i + 1) * TILE)
        g_buf[rows, :] = dot(x_ref[:, rows], dz_ref[...], TN).astype(BF16)
        pltpu.make_async_copy(g_buf.at[pl.ds(i * TILE, TILE), :], g_ref.at[pl.ds(i * TILE, TILE), :], out_sem).start()

    @pl.loop(0, 2 * FF // TILE, unroll=True)
    def _(i):
        rows = pl.ds(pl.multiple_of(i * (TILE // 2), TILE // 2), TILE // 2)
        part = dot(ht_ref[rows, :], dy_ref[...], NN)
        wire = pl.ds(pl.multiple_of(D + i * TILE, TILE), TILE)
        for c in range(WIDE // LANES):
            for half in range(2):
                first = half * HALF + c * LANES
                wide_ref[c, pl.ds(half, TILE // 2, 2), :] = part[:, first : first + LANES]
            g_buf[wire, c * LANES : (c + 1) * LANES] = wide_ref[c].astype(BF16)
        pltpu.make_async_copy(g_buf.at[wire, :], g_ref.at[wire, :], out_sem).start()

    pltpu.make_async_copy(g_buf, g_ref, out_sem).wait()
    dz_copy.wait()


def expert(step, counts, x, dy, weights):
    return pl.pallas_call(
        functools.partial(expert_kernel, step),
        out_shape=(
            jax.ShapeDtypeStruct(weights.shape, BF16),
            jax.ShapeDtypeStruct((ROWS, 2 * FF), BF16),
        ),
        in_specs=[in_hbm] * 4,
        out_specs=(in_hbm, in_hbm),
        scratch_shapes=[
            VMEM((ROWS, D), BF16),
            VMEM((ROWS, D), BF16),
            VMEM((ROWS, 2 * FF), BF16),
            VMEM((D, 2 * FF), BF16),
            VMEM((2 * FF, WIDE), BF16),
            VMEM((WIDE // LANES, TILE, LANES), F32),
            VMEM((FF, D), BF16),
            VMEM((ROWS, 2 * FF), F32),
            VMEM((ROWS, FF), F32),
            VMEM((ROWS, FF), BF16),
            VMEM((FF, ROWS), BF16),
            VMEM(weights.shape, BF16),
            SMEM(counts.shape, jnp.int32),
            pltpu.SemaphoreType.DMA((PARTS + 4,)),
            pltpu.SemaphoreType.DMA,
            pltpu.SemaphoreType.DMA,
        ],
        compiler_params=params(LIMIT),
        name="expert",
    )(counts, x, dy, weights)


def row_grad_kernel(dz_ref, w_ref, out_ref):
    out_ref[...] = dot(dz_ref[...], w_ref[...], NT).astype(BF16)


def row_grad(dz, weights):
    return pl.pallas_call(
        row_grad_kernel,
        grid=(D // TILE,),
        out_shape=jax.ShapeDtypeStruct((ROWS, D), BF16),
        in_specs=[
            pl.BlockSpec((ROWS, 2 * FF), lambda i: (0, 0)),
            pl.BlockSpec((TILE, WIDE), lambda i: (i, 0)),
        ],
        out_specs=pl.BlockSpec((ROWS, TILE), lambda i: (0, i)),
        compiler_params=params(32),
        cost_estimate=pl.CostEstimate(flops=2 * ROWS * D * 2 * FF, bytes_accessed=8 << 20, transcendentals=0),
        name="row_grad",
    )(dz, weights)


def sophia(grads, momentum, curvature, master):
    momentum = beta_one * momentum + (1.0 - beta_one) * grads
    curvature = beta_two * curvature + (1.0 - beta_two) * grads * grads
    master = master - learn_rate * jnp.clip(momentum / (rho_scale * curvature), -1.0, 1.0)
    return momentum, curvature, master


UNROLL = 2


def add_slots(places, place_ref, in_ref, buf_ref, acc_ref, sems):
    for copy in places:
        copy.start()


    def read(k):
        part = pl.ds(k * GROUP, GROUP)
        return pltpu.make_async_copy(in_ref.at[part], buf_ref.at[part], sems.at[k])

    groups = buf_ref.shape[0] // GROUP
    for k in range(groups):
        read(k).start()
    for acc in acc_ref:
        acc[...] = jnp.zeros_like(acc)
    for copy in places:
        copy.wait()

    @pl.loop(0, groups)
    def _(k):
        read(k).wait()

        @pl.loop(0, GROUP, step=2 * UNROLL)
        def _(i):
            for u in range(2 * UNROLL):
                d = k * GROUP + i + u
                acc = acc_ref[u % 2]
                rows = pl.ds(pl.multiple_of(expert_of(place_ref, d) * PIECE, 8), PIECE)
                for c in range(WIDE // LANES):
                    acc[c, rows, :] += buf_ref[d, :, c * LANES : (c + 1) * LANES].astype(F32)


def from_rows(acc_ref, j):
    parts = [acc_ref[c, pl.ds(j, EXPERTS, PIECE), :] for c in range(WIDE // LANES)]
    return jnp.concatenate(parts, axis=1)


def first_update_kernel(place_hbm, next_hbm, in_ref, m_ref, c_ref, w_ref, out_ref, *scratch):
    buf_ref, even_ref, odd_ref, bf_ref, m_buf, c_buf, w_buf = scratch[:7]
    place_ref, next_ref, place_sem, sems, state_sem, out_sem = scratch[7:]
    places = [
        pltpu.make_async_copy(place_hbm, place_ref, place_sem.at[0]),
        pltpu.make_async_copy(next_hbm, next_ref, place_sem.at[1]),
    ]
    state = [
        pltpu.make_async_copy(a, b, state_sem.at[i])
        for i, (a, b) in enumerate(((m_ref, m_buf), (c_ref, c_buf), (w_ref, w_buf)))
    ]
    for copy in state:
        copy.start()
    add_slots(places, place_ref, in_ref, buf_ref, (even_ref, odd_ref), sems)
    for copy in state:
        copy.wait()

    for j in range(PIECE):
        cols = slice(j * WIDE, (j + 1) * WIDE)
        grads = (from_rows(even_ref, j) + from_rows(odd_ref, j)) * grad_scale
        to_rows(sophia(grads, m_buf[:, cols], c_buf[:, cols], w_buf[:, cols])[2], j, even_ref)
    round_rows(even_ref, bf_ref)
    send_rows(next_ref, bf_ref, buf_ref, out_ref, out_sem)
    pltpu.make_async_copy(buf_ref, out_ref, out_sem).wait()


def first_update(place, next_place, arrived, momentum, curvature, master):
    dma = pltpu.SemaphoreType.DMA
    return pl.pallas_call(
        first_update_kernel,
        out_shape=jax.ShapeDtypeStruct(arrived.shape, BF16),
        in_specs=[in_hbm] * 6,
        out_specs=in_hbm,
        scratch_shapes=[VMEM(arrived.shape, BF16)]
        + [VMEM(ROW_STATE, F32)] * 2
        + [VMEM((EXPERTS, PIECE, WIDE), BF16)]
        + [VMEM(master.shape, F32)] * 3
        + [SMEM(place.shape, jnp.int32)] * 2
        + [dma((2,)), dma((arrived.shape[0] // GROUP,)), dma((3,)), dma],
        compiler_params=params(LIMIT),
        name="first_update",
    )(place, next_place, arrived, momentum, curvature, master)


def full_update_kernel(place_hbm, in_ref, m_ref, c_ref, w_ref, mo_ref, co_ref, wo_ref, *scratch):
    buf_ref, even_ref, odd_ref, m_buf, c_buf, w_buf, place_ref, place_sem, sems, state_sem, out_sem = scratch
    places = [pltpu.make_async_copy(place_hbm, place_ref, place_sem)]
    state = [
        pltpu.make_async_copy(a, b, state_sem.at[i])
        for i, (a, b) in enumerate(((m_ref, m_buf), (c_ref, c_buf), (w_ref, w_buf)))
    ]
    for copy in state:
        copy.start()
    add_slots(places, place_ref, in_ref, buf_ref, (even_ref, odd_ref), sems)
    for copy in state:
        copy.wait()
    for j in range(PIECE):
        cols = slice(j * WIDE, (j + 1) * WIDE)
        grads = (from_rows(even_ref, j) + from_rows(odd_ref, j)) * grad_scale
        values = sophia(grads, m_buf[:, cols], c_buf[:, cols], w_buf[:, cols])
        for i, (buf, out) in enumerate(((m_buf, mo_ref), (c_buf, co_ref), (w_buf, wo_ref))):
            buf[:, cols] = values[i]
            pltpu.make_async_copy(buf.at[:, cols], out.at[:, cols], out_sem.at[i]).start()
    for i, (buf, out) in enumerate(((m_buf, mo_ref), (c_buf, co_ref), (w_buf, wo_ref))):
        pltpu.make_async_copy(buf, out, out_sem.at[i]).wait()


def full_update(place, arrived, momentum, curvature, master):
    dma = pltpu.SemaphoreType.DMA
    return pl.pallas_call(
        full_update_kernel,
        out_shape=(jax.ShapeDtypeStruct(master.shape, F32),) * 3,
        in_specs=[in_hbm] * 5,
        out_specs=(in_hbm,) * 3,
        scratch_shapes=[VMEM(arrived.shape, BF16)]
        + [VMEM(ROW_STATE, F32)] * 2
        + [VMEM(master.shape, F32)] * 3
        + [SMEM(place.shape, jnp.int32)]
        + [dma, dma((arrived.shape[0] // GROUP,)), dma((3,)), dma((3,))],
        compiler_params=params(LIMIT),
        cost_estimate=pl.CostEstimate(flops=20 * master.size, bytes_accessed=16 << 20, transcendentals=0),
        name="full_update",
    )(place, arrived, momentum, curvature, master)


def exchange(blocks):
    return lax.all_to_all(blocks, ("slot", "grp"), 0, 0, tiled=True)


def body(token_rows, cotangents, row_counts, old_place, new_place, momentum, curvature, master):
    old_place, new_place = old_place.T, new_place.T
    x, dy = (v.reshape(-1, ROWS, D) for v in (token_rows, cotangents))
    counts = row_counts.reshape(-1)

    def slots(step, outgoing):
        arrived = exchange(outgoing)
        weights = arrived.reshape(-1, WIDE)
        grads, dz = expert(step, counts, x, dy, weights)
        return exchange(grads.reshape(arrived.shape)), row_grad(dz, weights)

    arrived, first_rows = slots(0, pack(old_place, master))
    outgoing = first_update(old_place, new_place, arrived, momentum, curvature, master)
    state = full_update(old_place, arrived, momentum, curvature, master)
    arrived, last_rows = slots(1, outgoing)
    state = full_update(new_place, arrived, *state)
    return (jnp.stack([first_rows, last_rows])[:, None, None], *state)


def solution(mesh):
    tokens = P(None, "slot", "grp", None, None)
    state = P(None, ("slot", "grp"))
    return jax.shard_map(
        body,
        mesh=mesh,
        in_specs=(tokens, tokens, P(None, "slot", "grp"), P(), P(), state, state, state),
        out_specs=(tokens, state, state, state),
        check_vma=False,
    )
```

```python
import functools

import jax
import jax.numpy as jnp
from jax import lax
from jax.experimental import pallas as pl
from jax.experimental.pallas import tpu as pltpu
from jax.sharding import PartitionSpec as P

D = 2048
FF = 512
ROWS = 384
WIDE = 1024
PIECE = 24
LANES = 128
EXPERTS = 16
LIMIT = 58
HALF = 1024

beta_one = 0.9
beta_two = 0.99
rho_scale = 2.0
learn_rate = 0.005
grad_scale = 0.25

F32 = jnp.float32
BF16 = jnp.bfloat16
VMEM = pltpu.VMEM
SMEM = pltpu.SMEM
in_hbm = pl.BlockSpec(memory_space=pl.ANY)

NT = (((1,), (1,)), ((), ()))
NN = (((1,), (0,)), ((), ()))
TN = (((0,), (0,)), ((), ()))


def params(limit_mb):
    return pltpu.CompilerParams(vmem_limit_bytes=limit_mb * 1024 * 1024)


def dot(a, b, dims):
    return lax.dot_general(a, b, dims, preferred_element_type=F32)


def expert_of(place_ref, d):
    groups = place_ref.shape[0]
    group = lax.rem(d, groups)
    return place_ref[group, lax.div(d, groups)] + group * (EXPERTS // groups)


def to_rows(values, j, rows_ref):
    for c in range(WIDE // LANES):
        rows_ref[c, pl.ds(j, values.shape[0], PIECE), :] = values[:, c * LANES : (c + 1) * LANES]


SPAN = 8
BATCH = 4
GROUP = 8


def round_rows(rows_ref, bf_ref):
    for c in range(WIDE // LANES):
        for e in range(EXPERTS):
            piece = rows_ref[c, e * PIECE : (e + 1) * PIECE, :]
            bf_ref[e, :, c * LANES : (c + 1) * LANES] = piece.astype(BF16)


def send_rows(place_ref, bf_ref, all_ref, out_ref, sem):
    @pl.loop(0, all_ref.shape[0] // GROUP)
    def _(k):
        @pl.loop(0, GROUP, unroll=8)
        def _(i):
            d = k * GROUP + i
            all_ref[d] = bf_ref[expert_of(place_ref, d)]

        part = pl.ds(k * GROUP, GROUP)
        pltpu.make_async_copy(all_ref.at[part], out_ref.at[part], sem).start()


ROW_STATE = (WIDE // LANES, EXPERTS * PIECE, LANES)


def pack_kernel(place_hbm, w_ref, out_ref, w_buf, rows_ref, bf_ref, all_ref, place_ref, in_sem, sem, place_sem):
    reads = []
    for k in range(PIECE // BATCH):
        cols = pl.ds(k * BATCH * WIDE, BATCH * WIDE)
        reads.append(pltpu.make_async_copy(w_ref.at[:, cols], w_buf.at[:, cols], in_sem.at[k]))
        reads[k].start()
    place_in = pltpu.make_async_copy(place_hbm, place_ref, place_sem)
    place_in.start()
    for j in range(PIECE):
        if j % BATCH == 0:
            reads[j // BATCH].wait()
        to_rows(w_buf[:, j * WIDE : (j + 1) * WIDE], j, rows_ref)
    round_rows(rows_ref, bf_ref)
    place_in.wait()
    send_rows(place_ref, bf_ref, all_ref, out_ref, sem)
    pltpu.make_async_copy(all_ref, out_ref, sem).wait()


def pack(place, master):
    return pl.pallas_call(
        pack_kernel,
        out_shape=jax.ShapeDtypeStruct((place.size, PIECE, WIDE), BF16),
        in_specs=[in_hbm] * 2,
        out_specs=in_hbm,
        scratch_shapes=[
            VMEM(master.shape, F32),
            VMEM(ROW_STATE, F32),
            VMEM((EXPERTS, PIECE, WIDE), BF16),
            VMEM((place.size, PIECE, WIDE), BF16),
            SMEM(place.shape, jnp.int32),
            pltpu.SemaphoreType.DMA((PIECE // BATCH,)),
            pltpu.SemaphoreType.DMA,
            pltpu.SemaphoreType.DMA,
        ],
        compiler_params=params(LIMIT),
        name="pack",
    )(place, master)


PARTS = 2
DEEP = D // PARTS
TILE = 256


def expert_kernel(step, count_hbm, x_hbm, dy_hbm, w_ref, g_ref, dz_out, *scratch):
    x_ref, dy_ref, dz_ref, wgu_ref, wire_ref, wide_ref, wd_ref = scratch[:7]
    z_ref, dh_ref, h_ref, ht_ref, g_buf, count_ref, in_sem, out_sem, dz_sem = scratch[7:]
    reads = []

    def read(source, target):
        reads.append(pltpu.make_async_copy(source, target, in_sem.at[len(reads)]))
        reads[-1].start()
        return reads[-1]

    down_in = read(w_ref.at[pl.ds(D, 2 * FF), :], wire_ref)
    dy_in = read(dy_hbm.at[step], dy_ref)
    x_in = read(x_hbm.at[step], x_ref)
    parts = []
    for k in range(PARTS):
        rows = pl.ds(k * DEEP, DEEP)
        parts.append(read(w_ref.at[rows, :], wgu_ref.at[rows, :]))

    count_in = read(count_hbm, count_ref)

    down_in.wait()
    for t in range(2 * FF // TILE):
        down = slice(t * TILE // 2, (t + 1) * TILE // 2)
        for c in range(WIDE // LANES):
            wide_ref[c] = wire_ref[t * TILE : (t + 1) * TILE, c * LANES : (c + 1) * LANES].astype(F32)
            for half in range(2):
                first = half * HALF + c * LANES
                wd_ref[down, first : first + LANES] = wide_ref[c, pl.ds(half, TILE // 2, 2), :].astype(BF16)
    dy_in.wait()
    for n in range(FF // TILE):
        cols = slice(n * TILE, (n + 1) * TILE)
        dh_ref[:, cols] = dot(dy_ref[...], wd_ref[cols, :], NT)
    count_in.wait()
    live = lax.broadcasted_iota(jnp.int32, (ROWS, TILE), 0) < count_ref[step]
    x_in.wait()
    for k in range(PARTS):
        parts[k].wait()
        rows = slice(k * DEEP, (k + 1) * DEEP)
        for n in range(FF // TILE):
            cols = slice(n * TILE, (n + 1) * TILE)
            ups = slice(FF + n * TILE, FF + (n + 1) * TILE)
            gate = dot(x_ref[:, rows], wgu_ref[rows, cols], NN)
            up = dot(x_ref[:, rows], wgu_ref[rows, ups], NN)
            if k > 0:
                gate, up = gate + z_ref[:, cols], up + z_ref[:, ups]
            if k < PARTS - 1:
                z_ref[:, cols], z_ref[:, ups] = gate, up
                continue
            dh = jnp.where(live, dh_ref[:, cols], 0.0)
            sig = jax.nn.sigmoid(gate)
            act = gate * sig
            slope = sig * (1.0 + gate * (1.0 - sig))
            h_ref[:, cols] = jnp.where(live, act * up, 0.0).astype(BF16)
            dz_ref[:, cols] = (dh * up * slope).astype(BF16)
            dz_ref[:, ups] = (dh * act).astype(BF16)
    dz_copy = pltpu.make_async_copy(dz_ref, dz_out, dz_sem)
    dz_copy.start()
    ht_ref[...] = h_ref[...].T

    for i in range(D // TILE):
        rows = slice(i * TILE, (i + 1) * TILE)
        g_buf[rows, :] = dot(x_ref[:, rows], dz_ref[...], TN).astype(BF16)
        pltpu.make_async_copy(g_buf.at[pl.ds(i * TILE, TILE), :], g_ref.at[pl.ds(i * TILE, TILE), :], out_sem).start()

    @pl.loop(0, 2 * FF // TILE, unroll=True)
    def _(i):
        rows = pl.ds(pl.multiple_of(i * (TILE // 2), TILE // 2), TILE // 2)
        part = dot(ht_ref[rows, :], dy_ref[...], NN)
        wire = pl.ds(pl.multiple_of(D + i * TILE, TILE), TILE)
        for c in range(WIDE // LANES):
            for half in range(2):
                first = half * HALF + c * LANES
                wide_ref[c, pl.ds(half, TILE // 2, 2), :] = part[:, first : first + LANES]
            g_buf[wire, c * LANES : (c + 1) * LANES] = wide_ref[c].astype(BF16)
        pltpu.make_async_copy(g_buf.at[wire, :], g_ref.at[wire, :], out_sem).start()

    pltpu.make_async_copy(g_buf, g_ref, out_sem).wait()
    dz_copy.wait()


def expert(step, counts, x, dy, weights):
    return pl.pallas_call(
        functools.partial(expert_kernel, step),
        out_shape=(
            jax.ShapeDtypeStruct(weights.shape, BF16),
            jax.ShapeDtypeStruct((ROWS, 2 * FF), BF16),
        ),
        in_specs=[in_hbm] * 4,
        out_specs=(in_hbm, in_hbm),
        scratch_shapes=[
            VMEM((ROWS, D), BF16),
            VMEM((ROWS, D), BF16),
            VMEM((ROWS, 2 * FF), BF16),
            VMEM((D, 2 * FF), BF16),
            VMEM((2 * FF, WIDE), BF16),
            VMEM((WIDE // LANES, TILE, LANES), F32),
            VMEM((FF, D), BF16),
            VMEM((ROWS, 2 * FF), F32),
            VMEM((ROWS, FF), F32),
            VMEM((ROWS, FF), BF16),
            VMEM((FF, ROWS), BF16),
            VMEM(weights.shape, BF16),
            SMEM(counts.shape, jnp.int32),
            pltpu.SemaphoreType.DMA((PARTS + 4,)),
            pltpu.SemaphoreType.DMA,
            pltpu.SemaphoreType.DMA,
        ],
        compiler_params=params(LIMIT),
        name="expert",
    )(counts, x, dy, weights)


def row_grad_kernel(dz_ref, w_ref, out_ref):
    out_ref[...] = dot(dz_ref[...], w_ref[...], NT).astype(BF16)


def row_grad(dz, weights):
    return pl.pallas_call(
        row_grad_kernel,
        grid=(D // TILE,),
        out_shape=jax.ShapeDtypeStruct((ROWS, D), BF16),
        in_specs=[
            pl.BlockSpec((ROWS, 2 * FF), lambda i: (0, 0)),
            pl.BlockSpec((TILE, WIDE), lambda i: (i, 0)),
        ],
        out_specs=pl.BlockSpec((ROWS, TILE), lambda i: (0, i)),
        compiler_params=params(32),
        cost_estimate=pl.CostEstimate(flops=2 * ROWS * D * 2 * FF, bytes_accessed=8 << 20, transcendentals=0),
        name="row_grad",
    )(dz, weights)


def sophia(grads, momentum, curvature, master):
    momentum = beta_one * momentum + (1.0 - beta_one) * grads
    curvature = beta_two * curvature + (1.0 - beta_two) * grads * grads
    master = master - learn_rate * jnp.clip(momentum / (rho_scale * curvature), -1.0, 1.0)
    return momentum, curvature, master


UNROLL = 2


def state_reads(pairs, sems):
    copies = []
    for k in range(PIECE // SPAN):
        cols = pl.ds(k * SPAN * WIDE, SPAN * WIDE)
        for i, (source, target) in enumerate(pairs):
            copies.append(pltpu.make_async_copy(source.at[:, cols], target.at[:, cols], sems.at[3 * k + i]))
    return copies


def add_slots(places, state, place_ref, in_ref, buf_ref, acc_ref, sems):
    for copy in places:
        copy.start()


    def read(k):
        part = pl.ds(k * GROUP, GROUP)
        return pltpu.make_async_copy(in_ref.at[part], buf_ref.at[part], sems.at[k])

    groups = buf_ref.shape[0] // GROUP
    for k in range(groups):
        read(k).start()
    for copy in state:
        copy.start()
    for acc in acc_ref:
        acc[...] = jnp.zeros_like(acc)
    for copy in places:
        copy.wait()

    @pl.loop(0, groups)
    def _(k):
        read(k).wait()

        @pl.loop(0, GROUP, step=2 * UNROLL)
        def _(i):
            for u in range(2 * UNROLL):
                d = k * GROUP + i + u
                acc = acc_ref[u % 2]
                rows = pl.ds(pl.multiple_of(expert_of(place_ref, d) * PIECE, 8), PIECE)
                for c in range(WIDE // LANES):
                    acc[c, rows, :] += buf_ref[d, :, c * LANES : (c + 1) * LANES].astype(F32)


def from_rows(acc_ref, j):
    parts = [acc_ref[c, pl.ds(j, EXPERTS, PIECE), :] for c in range(WIDE // LANES)]
    return jnp.concatenate(parts, axis=1)


def first_update_kernel(place_hbm, next_hbm, in_ref, m_ref, c_ref, w_ref, out_ref, *scratch):
    buf_ref, even_ref, odd_ref, bf_ref, m_buf, c_buf, w_buf = scratch[:7]
    place_ref, next_ref, place_sem, sems, state_sem, out_sem = scratch[7:]
    places = [
        pltpu.make_async_copy(place_hbm, place_ref, place_sem.at[0]),
        pltpu.make_async_copy(next_hbm, next_ref, place_sem.at[1]),
    ]
    state = state_reads(((m_ref, m_buf), (c_ref, c_buf), (w_ref, w_buf)), state_sem)
    add_slots(places, state, place_ref, in_ref, buf_ref, (even_ref, odd_ref), sems)

    for j in range(PIECE):
        cols = slice(j * WIDE, (j + 1) * WIDE)
        if j % SPAN == 0:
            for copy in state[3 * j // SPAN : 3 * j // SPAN + 3]:
                copy.wait()
        grads = (from_rows(even_ref, j) + from_rows(odd_ref, j)) * grad_scale
        to_rows(sophia(grads, m_buf[:, cols], c_buf[:, cols], w_buf[:, cols])[2], j, even_ref)
    round_rows(even_ref, bf_ref)
    send_rows(next_ref, bf_ref, buf_ref, out_ref, out_sem)
    pltpu.make_async_copy(buf_ref, out_ref, out_sem).wait()


def first_update(place, next_place, arrived, momentum, curvature, master):
    dma = pltpu.SemaphoreType.DMA
    return pl.pallas_call(
        first_update_kernel,
        out_shape=jax.ShapeDtypeStruct(arrived.shape, BF16),
        in_specs=[in_hbm] * 6,
        out_specs=in_hbm,
        scratch_shapes=[VMEM(arrived.shape, BF16)]
        + [VMEM(ROW_STATE, F32)] * 2
        + [VMEM((EXPERTS, PIECE, WIDE), BF16)]
        + [VMEM(master.shape, F32)] * 3
        + [SMEM(place.shape, jnp.int32)] * 2
        + [dma((2,)), dma((arrived.shape[0] // GROUP,)), dma((3 * PIECE // SPAN,)), dma],
        compiler_params=params(LIMIT),
        name="first_update",
    )(place, next_place, arrived, momentum, curvature, master)


def full_update_kernel(place_hbm, in_ref, m_ref, c_ref, w_ref, mo_ref, co_ref, wo_ref, *scratch):
    buf_ref, even_ref, odd_ref, m_buf, c_buf, w_buf, place_ref, place_sem, sems, state_sem, out_sem = scratch
    places = [pltpu.make_async_copy(place_hbm, place_ref, place_sem)]
    state = state_reads(((m_ref, m_buf), (c_ref, c_buf), (w_ref, w_buf)), state_sem)
    add_slots(places, state, place_ref, in_ref, buf_ref, (even_ref, odd_ref), sems)
    for j in range(PIECE):
        cols = slice(j * WIDE, (j + 1) * WIDE)
        if j % SPAN == 0:
            for copy in state[3 * j // SPAN : 3 * j // SPAN + 3]:
                copy.wait()
        grads = (from_rows(even_ref, j) + from_rows(odd_ref, j)) * grad_scale
        values = sophia(grads, m_buf[:, cols], c_buf[:, cols], w_buf[:, cols])
        for i, (buf, out) in enumerate(((m_buf, mo_ref), (c_buf, co_ref), (w_buf, wo_ref))):
            buf[:, cols] = values[i]
            pltpu.make_async_copy(buf.at[:, cols], out.at[:, cols], out_sem.at[i]).start()
    for i, (buf, out) in enumerate(((m_buf, mo_ref), (c_buf, co_ref), (w_buf, wo_ref))):
        pltpu.make_async_copy(buf, out, out_sem.at[i]).wait()


def full_update(place, arrived, momentum, curvature, master):
    dma = pltpu.SemaphoreType.DMA
    return pl.pallas_call(
        full_update_kernel,
        out_shape=(jax.ShapeDtypeStruct(master.shape, F32),) * 3,
        in_specs=[in_hbm] * 5,
        out_specs=(in_hbm,) * 3,
        scratch_shapes=[VMEM(arrived.shape, BF16)]
        + [VMEM(ROW_STATE, F32)] * 2
        + [VMEM(master.shape, F32)] * 3
        + [SMEM(place.shape, jnp.int32)]
        + [dma, dma((arrived.shape[0] // GROUP,)), dma((3 * PIECE // SPAN,)), dma((3,))],
        compiler_params=params(LIMIT),
        cost_estimate=pl.CostEstimate(flops=20 * master.size, bytes_accessed=16 << 20, transcendentals=0),
        name="full_update",
    )(place, arrived, momentum, curvature, master)


def exchange(blocks):
    return lax.all_to_all(blocks, ("slot", "grp"), 0, 0, tiled=True)


def body(token_rows, cotangents, row_counts, old_place, new_place, momentum, curvature, master):
    old_place, new_place = old_place.T, new_place.T
    x, dy = (v.reshape(-1, ROWS, D) for v in (token_rows, cotangents))
    counts = row_counts.reshape(-1)

    def slots(step, outgoing):
        arrived = exchange(outgoing)
        weights = arrived.reshape(-1, WIDE)
        grads, dz = expert(step, counts, x, dy, weights)
        return exchange(grads.reshape(arrived.shape)), row_grad(dz, weights)

    arrived, first_rows = slots(0, pack(old_place, master))
    outgoing = first_update(old_place, new_place, arrived, momentum, curvature, master)
    state = full_update(old_place, arrived, momentum, curvature, master)
    arrived, last_rows = slots(1, outgoing)
    state = full_update(new_place, arrived, *state)
    return (jnp.stack([first_rows, last_rows])[:, None, None], *state)


def solution(mesh):
    tokens = P(None, "slot", "grp", None, None)
    state = P(None, ("slot", "grp"))
    return jax.shard_map(
        body,
        mesh=mesh,
        in_specs=(tokens, tokens, P(None, "slot", "grp"), P(), P(), state, state, state),
        out_specs=(tokens, state, state, state),
        check_vma=False,
    )
```

```python
import functools

import jax
import jax.numpy as jnp
from jax import lax
from jax.experimental import pallas as pl
from jax.experimental.pallas import tpu as pltpu
from jax.sharding import PartitionSpec as P

D = 2048
FF = 512
ROWS = 384
WIDE = 1024
PIECE = 24
LANES = 128
EXPERTS = 16
LIMIT = 58
HALF = 1024

beta_one = 0.9
beta_two = 0.99
rho_scale = 2.0
learn_rate = 0.005
grad_scale = 0.25

F32 = jnp.float32
BF16 = jnp.bfloat16
VMEM = pltpu.VMEM
SMEM = pltpu.SMEM
in_hbm = pl.BlockSpec(memory_space=pl.ANY)

NT = (((1,), (1,)), ((), ()))
NN = (((1,), (0,)), ((), ()))
TN = (((0,), (0,)), ((), ()))


def params(limit_mb):
    return pltpu.CompilerParams(vmem_limit_bytes=limit_mb * 1024 * 1024)


def dot(a, b, dims):
    return lax.dot_general(a, b, dims, preferred_element_type=F32)


def expert_of(place_ref, d):
    groups = place_ref.shape[0]
    group = lax.rem(d, groups)
    return place_ref[group, lax.div(d, groups)] + group * (EXPERTS // groups)


def to_rows(values, j, rows_ref):
    for c in range(WIDE // LANES):
        rows_ref[c, pl.ds(j, values.shape[0], PIECE), :] = values[:, c * LANES : (c + 1) * LANES]


SPAN = 8
LAST_SPAN = 12
BATCH = 4
GROUP = 8


def round_rows(rows_ref, bf_ref):
    for c in range(WIDE // LANES):
        for e in range(EXPERTS):
            piece = rows_ref[c, e * PIECE : (e + 1) * PIECE, :]
            bf_ref[e, :, c * LANES : (c + 1) * LANES] = piece.astype(BF16)


def send_rows(place_ref, bf_ref, all_ref, out_ref, sem):
    @pl.loop(0, all_ref.shape[0] // GROUP)
    def _(k):
        @pl.loop(0, GROUP, unroll=8)
        def _(i):
            d = k * GROUP + i
            all_ref[d] = bf_ref[expert_of(place_ref, d)]

        part = pl.ds(k * GROUP, GROUP)
        pltpu.make_async_copy(all_ref.at[part], out_ref.at[part], sem).start()


ROW_STATE = (WIDE // LANES, EXPERTS * PIECE, LANES)


def pack_kernel(place_hbm, w_ref, out_ref, w_buf, rows_ref, bf_ref, all_ref, place_ref, in_sem, sem, place_sem):
    reads = []
    for k in range(PIECE // BATCH):
        cols = pl.ds(k * BATCH * WIDE, BATCH * WIDE)
        reads.append(pltpu.make_async_copy(w_ref.at[:, cols], w_buf.at[:, cols], in_sem.at[k]))
        reads[k].start()
    place_in = pltpu.make_async_copy(place_hbm, place_ref, place_sem)
    place_in.start()
    for j in range(PIECE):
        if j % BATCH == 0:
            reads[j // BATCH].wait()
        to_rows(w_buf[:, j * WIDE : (j + 1) * WIDE], j, rows_ref)
    round_rows(rows_ref, bf_ref)
    place_in.wait()
    send_rows(place_ref, bf_ref, all_ref, out_ref, sem)
    pltpu.make_async_copy(all_ref, out_ref, sem).wait()


def pack(place, master):
    return pl.pallas_call(
        pack_kernel,
        out_shape=jax.ShapeDtypeStruct((place.size, PIECE, WIDE), BF16),
        in_specs=[in_hbm] * 2,
        out_specs=in_hbm,
        scratch_shapes=[
            VMEM(master.shape, F32),
            VMEM(ROW_STATE, F32),
            VMEM((EXPERTS, PIECE, WIDE), BF16),
            VMEM((place.size, PIECE, WIDE), BF16),
            SMEM(place.shape, jnp.int32),
            pltpu.SemaphoreType.DMA((PIECE // BATCH,)),
            pltpu.SemaphoreType.DMA,
            pltpu.SemaphoreType.DMA,
        ],
        compiler_params=params(LIMIT),
        name="pack",
    )(place, master)


PARTS = 2
DEEP = D // PARTS
TILE = 256


def expert_kernel(step, count_hbm, x_hbm, dy_hbm, w_ref, g_ref, dz_out, *scratch):
    x_ref, dy_ref, dz_ref, wgu_ref, wire_ref, wide_ref, wd_ref = scratch[:7]
    z_ref, dh_ref, h_ref, ht_ref, g_buf, count_ref, in_sem, out_sem, dz_sem = scratch[7:]
    reads = []

    def read(source, target):
        reads.append(pltpu.make_async_copy(source, target, in_sem.at[len(reads)]))
        reads[-1].start()
        return reads[-1]

    down_in = read(w_ref.at[pl.ds(D, 2 * FF), :], wire_ref)
    dy_in = read(dy_hbm.at[step], dy_ref)
    x_in = read(x_hbm.at[step], x_ref)
    parts = []
    for k in range(PARTS):
        rows = pl.ds(k * DEEP, DEEP)
        parts.append(read(w_ref.at[rows, :], wgu_ref.at[rows, :]))

    count_in = read(count_hbm, count_ref)

    down_in.wait()
    for t in range(2 * FF // TILE):
        down = slice(t * TILE // 2, (t + 1) * TILE // 2)
        for c in range(WIDE // LANES):
            wide_ref[c] = wire_ref[t * TILE : (t + 1) * TILE, c * LANES : (c + 1) * LANES].astype(F32)
            for half in range(2):
                first = half * HALF + c * LANES
                wd_ref[down, first : first + LANES] = wide_ref[c, pl.ds(half, TILE // 2, 2), :].astype(BF16)
    dy_in.wait()
    for n in range(FF // TILE):
        cols = slice(n * TILE, (n + 1) * TILE)
        dh_ref[:, cols] = dot(dy_ref[...], wd_ref[cols, :], NT)
    count_in.wait()
    live = lax.broadcasted_iota(jnp.int32, (ROWS, TILE), 0) < count_ref[step]
    x_in.wait()
    for k in range(PARTS):
        parts[k].wait()
        rows = slice(k * DEEP, (k + 1) * DEEP)
        for n in range(FF // TILE):
            cols = slice(n * TILE, (n + 1) * TILE)
            ups = slice(FF + n * TILE, FF + (n + 1) * TILE)
            gate = dot(x_ref[:, rows], wgu_ref[rows, cols], NN)
            up = dot(x_ref[:, rows], wgu_ref[rows, ups], NN)
            if k > 0:
                gate, up = gate + z_ref[:, cols], up + z_ref[:, ups]
            if k < PARTS - 1:
                z_ref[:, cols], z_ref[:, ups] = gate, up
                continue
            dh = jnp.where(live, dh_ref[:, cols], 0.0)
            sig = jax.nn.sigmoid(gate)
            act = gate * sig
            slope = sig * (1.0 + gate * (1.0 - sig))
            h_ref[:, cols] = jnp.where(live, act * up, 0.0).astype(BF16)
            dz_ref[:, cols] = (dh * up * slope).astype(BF16)
            dz_ref[:, ups] = (dh * act).astype(BF16)
    dz_copy = pltpu.make_async_copy(dz_ref, dz_out, dz_sem)
    dz_copy.start()
    ht_ref[...] = h_ref[...].T

    for i in range(D // TILE):
        rows = slice(i * TILE, (i + 1) * TILE)
        g_buf[rows, :] = dot(x_ref[:, rows], dz_ref[...], TN).astype(BF16)
        pltpu.make_async_copy(g_buf.at[pl.ds(i * TILE, TILE), :], g_ref.at[pl.ds(i * TILE, TILE), :], out_sem).start()

    @pl.loop(0, 2 * FF // TILE, unroll=True)
    def _(i):
        rows = pl.ds(pl.multiple_of(i * (TILE // 2), TILE // 2), TILE // 2)
        part = dot(ht_ref[rows, :], dy_ref[...], NN)
        wire = pl.ds(pl.multiple_of(D + i * TILE, TILE), TILE)
        for c in range(WIDE // LANES):
            for half in range(2):
                first = half * HALF + c * LANES
                wide_ref[c, pl.ds(half, TILE // 2, 2), :] = part[:, first : first + LANES]
            g_buf[wire, c * LANES : (c + 1) * LANES] = wide_ref[c].astype(BF16)
        pltpu.make_async_copy(g_buf.at[wire, :], g_ref.at[wire, :], out_sem).start()

    pltpu.make_async_copy(g_buf, g_ref, out_sem).wait()
    dz_copy.wait()


def expert(step, counts, x, dy, weights):
    return pl.pallas_call(
        functools.partial(expert_kernel, step),
        out_shape=(
            jax.ShapeDtypeStruct(weights.shape, BF16),
            jax.ShapeDtypeStruct((ROWS, 2 * FF), BF16),
        ),
        in_specs=[in_hbm] * 4,
        out_specs=(in_hbm, in_hbm),
        scratch_shapes=[
            VMEM((ROWS, D), BF16),
            VMEM((ROWS, D), BF16),
            VMEM((ROWS, 2 * FF), BF16),
            VMEM((D, 2 * FF), BF16),
            VMEM((2 * FF, WIDE), BF16),
            VMEM((WIDE // LANES, TILE, LANES), F32),
            VMEM((FF, D), BF16),
            VMEM((ROWS, 2 * FF), F32),
            VMEM((ROWS, FF), F32),
            VMEM((ROWS, FF), BF16),
            VMEM((FF, ROWS), BF16),
            VMEM(weights.shape, BF16),
            SMEM(counts.shape, jnp.int32),
            pltpu.SemaphoreType.DMA((PARTS + 4,)),
            pltpu.SemaphoreType.DMA,
            pltpu.SemaphoreType.DMA,
        ],
        compiler_params=params(LIMIT),
        name="expert",
    )(counts, x, dy, weights)


def row_grad_kernel(dz_ref, w_ref, out_ref):
    out_ref[...] = dot(dz_ref[...], w_ref[...], NT).astype(BF16)


def row_grad(dz, weights):
    return pl.pallas_call(
        row_grad_kernel,
        grid=(D // TILE,),
        out_shape=jax.ShapeDtypeStruct((ROWS, D), BF16),
        in_specs=[
            pl.BlockSpec((ROWS, 2 * FF), lambda i: (0, 0)),
            pl.BlockSpec((TILE, WIDE), lambda i: (i, 0)),
        ],
        out_specs=pl.BlockSpec((ROWS, TILE), lambda i: (0, i)),
        compiler_params=params(32),
        cost_estimate=pl.CostEstimate(flops=2 * ROWS * D * 2 * FF, bytes_accessed=8 << 20, transcendentals=0),
        name="row_grad",
    )(dz, weights)


def sophia(grads, momentum, curvature, master):
    momentum = beta_one * momentum + (1.0 - beta_one) * grads
    curvature = beta_two * curvature + (1.0 - beta_two) * grads * grads
    master = master - learn_rate * jnp.clip(momentum / (rho_scale * curvature), -1.0, 1.0)
    return momentum, curvature, master


UNROLL = 2


def state_reads(pairs, sems, span):
    copies = []
    for k in range(PIECE // span):
        cols = pl.ds(k * span * WIDE, span * WIDE)
        for i, (source, target) in enumerate(pairs):
            copies.append(pltpu.make_async_copy(source.at[:, cols], target.at[:, cols], sems.at[3 * k + i]))
    return copies


def add_slots(places, state, place_ref, in_ref, buf_ref, acc_ref, sems):
    for copy in places:
        copy.start()


    def read(k):
        part = pl.ds(k * GROUP, GROUP)
        return pltpu.make_async_copy(in_ref.at[part], buf_ref.at[part], sems.at[k])

    groups = buf_ref.shape[0] // GROUP
    for k in range(groups):
        read(k).start()
    for copy in state:
        copy.start()
    for acc in acc_ref:
        acc[...] = jnp.zeros_like(acc)
    for copy in places:
        copy.wait()

    @pl.loop(0, groups)
    def _(k):
        read(k).wait()

        @pl.loop(0, GROUP, step=2 * UNROLL)
        def _(i):
            for u in range(2 * UNROLL):
                d = k * GROUP + i + u
                acc = acc_ref[u % 2]
                rows = pl.ds(pl.multiple_of(expert_of(place_ref, d) * PIECE, 8), PIECE)
                for c in range(WIDE // LANES):
                    acc[c, rows, :] += buf_ref[d, :, c * LANES : (c + 1) * LANES].astype(F32)


def from_rows(acc_ref, j):
    parts = [acc_ref[c, pl.ds(j, EXPERTS, PIECE), :] for c in range(WIDE // LANES)]
    return jnp.concatenate(parts, axis=1)


def first_update_kernel(place_hbm, next_hbm, in_ref, m_ref, c_ref, w_ref, out_ref, *scratch):
    buf_ref, even_ref, odd_ref, bf_ref, m_buf, c_buf, w_buf = scratch[:7]
    place_ref, next_ref, place_sem, sems, state_sem, out_sem = scratch[7:]
    places = [
        pltpu.make_async_copy(place_hbm, place_ref, place_sem.at[0]),
        pltpu.make_async_copy(next_hbm, next_ref, place_sem.at[1]),
    ]
    state = state_reads(((m_ref, m_buf), (c_ref, c_buf), (w_ref, w_buf)), state_sem, SPAN)
    add_slots(places, state, place_ref, in_ref, buf_ref, (even_ref, odd_ref), sems)

    for j in range(PIECE):
        cols = slice(j * WIDE, (j + 1) * WIDE)
        if j % SPAN == 0:
            for copy in state[3 * j // SPAN : 3 * j // SPAN + 3]:
                copy.wait()
        grads = (from_rows(even_ref, j) + from_rows(odd_ref, j)) * grad_scale
        to_rows(sophia(grads, m_buf[:, cols], c_buf[:, cols], w_buf[:, cols])[2], j, even_ref)
    round_rows(even_ref, bf_ref)
    send_rows(next_ref, bf_ref, buf_ref, out_ref, out_sem)
    pltpu.make_async_copy(buf_ref, out_ref, out_sem).wait()


def first_update(place, next_place, arrived, momentum, curvature, master):
    dma = pltpu.SemaphoreType.DMA
    return pl.pallas_call(
        first_update_kernel,
        out_shape=jax.ShapeDtypeStruct(arrived.shape, BF16),
        in_specs=[in_hbm] * 6,
        out_specs=in_hbm,
        scratch_shapes=[VMEM(arrived.shape, BF16)]
        + [VMEM(ROW_STATE, F32)] * 2
        + [VMEM((EXPERTS, PIECE, WIDE), BF16)]
        + [VMEM(master.shape, F32)] * 3
        + [SMEM(place.shape, jnp.int32)] * 2
        + [dma((2,)), dma((arrived.shape[0] // GROUP,)), dma((3 * PIECE // SPAN,)), dma],
        compiler_params=params(LIMIT),
        name="first_update",
    )(place, next_place, arrived, momentum, curvature, master)


def full_update_kernel(place_hbm, in_ref, m_ref, c_ref, w_ref, mo_ref, co_ref, wo_ref, *scratch):
    buf_ref, even_ref, odd_ref, m_buf, c_buf, w_buf, place_ref, place_sem, sems, state_sem, out_sem = scratch
    places = [pltpu.make_async_copy(place_hbm, place_ref, place_sem)]
    state = state_reads(((m_ref, m_buf), (c_ref, c_buf), (w_ref, w_buf)), state_sem, LAST_SPAN)
    add_slots(places, state, place_ref, in_ref, buf_ref, (even_ref, odd_ref), sems)
    for j in range(PIECE):
        cols = slice(j * WIDE, (j + 1) * WIDE)
        if j % LAST_SPAN == 0:
            for copy in state[3 * j // LAST_SPAN : 3 * j // LAST_SPAN + 3]:
                copy.wait()
        grads = (from_rows(even_ref, j) + from_rows(odd_ref, j)) * grad_scale
        values = sophia(grads, m_buf[:, cols], c_buf[:, cols], w_buf[:, cols])
        for i, (buf, out) in enumerate(((m_buf, mo_ref), (c_buf, co_ref), (w_buf, wo_ref))):
            buf[:, cols] = values[i]
            pltpu.make_async_copy(buf.at[:, cols], out.at[:, cols], out_sem.at[i]).start()
    for i, (buf, out) in enumerate(((m_buf, mo_ref), (c_buf, co_ref), (w_buf, wo_ref))):
        pltpu.make_async_copy(buf, out, out_sem.at[i]).wait()


def full_update(place, arrived, momentum, curvature, master):
    dma = pltpu.SemaphoreType.DMA
    return pl.pallas_call(
        full_update_kernel,
        out_shape=(jax.ShapeDtypeStruct(master.shape, F32),) * 3,
        in_specs=[in_hbm] * 5,
        out_specs=(in_hbm,) * 3,
        scratch_shapes=[VMEM(arrived.shape, BF16)]
        + [VMEM(ROW_STATE, F32)] * 2
        + [VMEM(master.shape, F32)] * 3
        + [SMEM(place.shape, jnp.int32)]
        + [dma, dma((arrived.shape[0] // GROUP,)), dma((3 * PIECE // LAST_SPAN,)), dma((3,))],
        compiler_params=params(LIMIT),
        cost_estimate=pl.CostEstimate(flops=20 * master.size, bytes_accessed=16 << 20, transcendentals=0),
        name="full_update",
    )(place, arrived, momentum, curvature, master)


def exchange(blocks):
    return lax.all_to_all(blocks, ("slot", "grp"), 0, 0, tiled=True)


def body(token_rows, cotangents, row_counts, old_place, new_place, momentum, curvature, master):
    old_place, new_place = old_place.T, new_place.T
    x, dy = (v.reshape(-1, ROWS, D) for v in (token_rows, cotangents))
    counts = row_counts.reshape(-1)

    def slots(step, outgoing):
        arrived = exchange(outgoing)
        weights = arrived.reshape(-1, WIDE)
        grads, dz = expert(step, counts, x, dy, weights)
        return exchange(grads.reshape(arrived.shape)), row_grad(dz, weights)

    arrived, first_rows = slots(0, pack(old_place, master))
    outgoing = first_update(old_place, new_place, arrived, momentum, curvature, master)
    state = full_update(old_place, arrived, momentum, curvature, master)
    arrived, last_rows = slots(1, outgoing)
    state = full_update(new_place, arrived, *state)
    return (jnp.stack([first_rows, last_rows])[:, None, None], *state)


def solution(mesh):
    tokens = P(None, "slot", "grp", None, None)
    state = P(None, ("slot", "grp"))
    return jax.shard_map(
        body,
        mesh=mesh,
        in_specs=(tokens, tokens, P(None, "slot", "grp"), P(), P(), state, state, state),
        out_specs=(tokens, state, state, state),
        check_vma=False,
    )
```
